128 devices in a mesh: row: 16 (over z_lo, y, core), col: 8 (over z_hi, x).
Axes of the slice: x: 4, y: 4, z: 4 (z_hi: 2, z_lo: 2; z = z_hi * 2 + z_lo), core: 2. Of those that a mesh axis runs over, the one named last changes fastest.
Arguments:
- teacher: bfloat16 [24576, 512], P(('row', 'col')), may hold values from -2.5 to 2.5
- student: bfloat16 [24576, 512], P(('row', 'col')), may hold values from -2.5 to 2.5
Outputs:
- grad_student: float32 [24576, 512], P(('row', 'col'))
The draws below stay inside these ranges and needn't reach their ends.
All inputs are finite; a program needn't handle non-finite values.
Results may differ from the reference program's by a relative error of at most 0.0017.
Values may be sent and summed in bfloat16 or wider, within the bound.
A program may use at most 64 MiB of HBM per device.

```python
import math
import jax
import jax.numpy as jnp
from jax import lax

D = 512
BATCH = 24576


def normal_rows(key):
    return 0.5 * jnp.clip(jax.random.normal(key, (BATCH, D), jnp.float32), -5.0, 5.0)


def draw_teacher(key, part):
    return normal_rows(key).astype(jnp.bfloat16)


def draw_student(key, part):
    shared = normal_rows(key)
    key = jax.random.fold_in(key, 5)
    mixed = jnp.clip(0.6 * shared + 0.8 * normal_rows(key), -2.5, 2.5)
    return mixed.astype(jnp.bfloat16)


def setup_inputs(seed: int = 0) -> dict:
    key_of = jax.random.split(jax.random.key(seed), 3)
    teacher = draw_teacher(jax.random.fold_in(key_of[2], 71), 0)
    student = draw_student(jax.random.fold_in(key_of[2], 71), 0)
    return dict(teacher=teacher, student=student)


def reference(teacher, student):
    total = teacher.shape[0]
    width = teacher.shape[1]
    scale = 1.0 / (0.1 * math.sqrt(width))
    block = math.gcd(total, 1024)
    every = jnp.arange(total, dtype=jnp.int32)
    starts = jnp.arange(total // block, dtype=jnp.int32) * block

    def one(carry, start):
        rows_t = lax.dynamic_slice_in_dim(teacher, start, block, 0)
        rows_s = lax.dynamic_slice_in_dim(student, start, block, 0)
        dims = (((1,), (1,)), ((), ()))
        zt = lax.dot_general(rows_t, teacher, dims, preferred_element_type=jnp.float32) * scale
        zs = lax.dot_general(rows_s, student, dims, preferred_element_type=jnp.float32) * scale
        self_pair = (start + jnp.arange(block, dtype=jnp.int32))[:, None] == every[None, :]
        zt = jnp.where(self_pair, -1e+30, zt)
        zs = jnp.where(self_pair, -1e+30, zs)
        top_t = lax.optimization_barrier(jnp.max(zt, axis=1, keepdims=True))
        top_s = lax.optimization_barrier(jnp.max(zs, axis=1, keepdims=True))
        exp_t = jnp.exp(zt - top_t)
        exp_s = jnp.exp(zs - top_s)
        gdiff = (exp_s / lax.optimization_barrier(jnp.sum(exp_s, axis=1, keepdims=True)) - exp_t / lax.optimization_barrier(jnp.sum(exp_t, axis=1, keepdims=True))).astype(jnp.bfloat16)
        forward = jnp.dot(gdiff, student, preferred_element_type=jnp.float32)
        backward = lax.dot_general(gdiff, rows_s, (((0,), (0,)), ((), ())), preferred_element_type=jnp.float32)
        return (carry + backward, forward)
    backward, forward = lax.scan(one, jnp.zeros((total, width), jnp.float32), starts)
    return scale * (forward.reshape(total, width) + backward)
```

```python
import math

import jax
import jax.numpy as jnp
from jax import lax
from jax.experimental import pallas as pl
from jax.experimental.pallas import tpu as pltpu
from jax.sharding import PartitionSpec as P

F32 = jnp.float32
BF16 = jnp.bfloat16
MESH = pl.DeviceIdType.MESH
SIDE = 4

OFFSETS = (
    (0, 0, 0), (3, 0, 0), (0, 0, 1), (1, 0, 0), (0, 3, 3), (3, 1, 0),
    (1, 0, 1), (0, 2, 3), (3, 2, 0), (3, 1, 3), (1, 0, 2),
)
PARENT = (None, 0, 0, 0, 0, 1, 2, 4, 5, 5, 6)
SLOTS = len(OFFSETS)
CHILDREN = tuple(tuple(q for q in range(SLOTS) if PARENT[q] == p) for p in range(SLOTS))
ARRIVALS = (
    (0, 0), (0, 1), (2, 0), (1, 0), (4, 0), (3, 0), (2, 1), (1, 1), (4, 1), (3, 1),
    (6, 0), (5, 0), (7, 0), (6, 1), (5, 1), (7, 1), (10, 0), (8, 0), (9, 0), (10, 1), (8, 1), (9, 1),
)


def minus(a, b):
    return tuple((p - q) % SIDE for p, q in zip(a, b))


def work_lists():
    found, pairs = set(), [(0, 0, 1)]
    for j in range(SLOTS):
        for i in range(j):
            d = minus(OFFSETS[j], OFFSETS[i])
            e = minus((0, 0, 0), d)
            if min(d, e) not in found:
                found.add(min(d, e))
                pairs.append((i, j, int(d == e)))
    assert len(found) == (SIDE**3 - 1 + 7) // 2
    cores = ([], [])
    for kind in (0, 1):
        for n, pair in enumerate(p for p in pairs if p[2] == kind):
            cores[(n + kind) % 2].append(pair)
    return tuple(sorted(c, key=lambda p: (max(p[:2]), p)) for c in cores)


WORK = work_lists()
STEPS = len(WORK[0])


def last_slot(n):
    return max(max(WORK[core][m][:2]) for core in (0, 1) for m in range(n + 1))


def first_use(q):
    return min(n for core in (0, 1) for n in range(STEPS) if q in WORK[core][n][:2])


def table(core, n, field):
    value = jnp.int32(0)
    for m in range(STEPS):
        one, two = WORK[0][m][field], WORK[1][m][field]
        if one == two:
            entry = jnp.int32(one)
        else:
            entry = jnp.where(core == 0, jnp.int32(one), jnp.int32(two))
        value = jnp.where(n == m, entry, value)
    return value


def kernel(
    t_ref, s_ref, o_ref, rows, z, acc, stat, stat_in, both, both_in, norm, half_in, part_in,
    tree_send, tree_recv, pair_send, pair_recv, stat_send, stat_recv, both_send, both_recv,
    norm_send, norm_recv, half_send, half_recv, part_send, part_recv,
):
    shard, width = t_ref.shape
    full = 2 * shard
    scale = 1.0 / (0.1 * math.sqrt(width))
    row = lax.axis_index("row")
    col = lax.axis_index("col")
    core = lax.rem(row, 2)
    other = 1 - core
    y = lax.rem(lax.div(row, 2), SIDE)
    x = lax.rem(col, SIDE)
    zz = lax.div(col, SIDE) * 2 + lax.div(row, 2 * SIDE)

    def device(d, to_core, sign=1):
        at = [lax.rem(p + (sign * q) % SIDE, SIDE) for p, q in zip((x, y, zz), d)]
        return (
            (lax.rem(at[2], 2) * SIDE + at[1]) * 2 + to_core,
            lax.div(at[2], 2) * SIDE + at[0],
        )

    sibling = (lax.div(row, 2) * 2 + other, col)

    def edge(q):
        return minus(OFFSETS[q], OFFSETS[PARENT[q]])

    partners = set()
    for q in range(1, SLOTS):
        for d in (OFFSETS[q], edge(q)):
            partners.add(d)
            partners.add(minus((0, 0, 0), d))
    partners = sorted(partners)

    barrier = pltpu.get_barrier_semaphore()
    for d in partners:
        pl.semaphore_signal(barrier, inc=1, device_id=device(d, core), device_id_type=MESH)
    pl.semaphore_signal(barrier, inc=1, device_id=sibling, device_id_type=MESH)
    rows[0, 0, core] = t_ref[...]
    rows[0, 1, core] = s_ref[...]
    pl.semaphore_wait(barrier, len(partners) + 1)

    def remote(src, dst, send, recv, to):
        return pltpu.make_async_remote_copy(
            src_ref=src, dst_ref=dst, send_sem=send, recv_sem=recv, device_id=to, device_id_type=MESH
        )

    def tree(q, m):
        return remote(
            rows.at[PARENT[q], m, core], rows.at[q, m, core], tree_send.at[q, m], tree_recv.at[q, m],
            device(edge(q), core, -1),
        )

    def across(q, m):
        return remote(
            rows.at[q, m, core], rows.at[q, m, core], pair_send.at[q, m], pair_recv.at[q, m], sibling
        )

    def take_up(q, m):
        if q:
            tree(q, m).wait_recv()
        for child in CHILDREN[q]:
            tree(child, m).start()
        across(q, m).start()

    for q, m in ARRIVALS[:2]:
        take_up(q, m)

    acc[...] = jnp.zeros_like(acc)
    for m in range(2):
        stat[:, 2 * m : 2 * m + 1, :] = jnp.full((SLOTS, 1, full), -1e30, F32)
        stat[:, 2 * m + 1 : 2 * m + 2, :] = jnp.zeros((SLOTS, 1, full), F32)

    def block(q, m):
        return rows[q, m].reshape(full, width)

    def as_row(column):
        return jnp.transpose(jnp.broadcast_to(column, (full, 128)))[0:1]

    def as_column(line):
        wide = jnp.transpose(jnp.broadcast_to(line, (128, full)))
        return jnp.concatenate([wide] * (full // 128), axis=1)

    def merge(ref, m, top, total):
        old = ref[2 * m : 2 * m + 1, :]
        new = jnp.maximum(old, top)
        ref[2 * m + 1 : 2 * m + 2, :] = ref[2 * m + 1 : 2 * m + 2, :] * jnp.exp2(
            old - new
        ) + total * jnp.exp2(top - new)
        ref[2 * m : 2 * m + 1, :] = new

    def first_pass(n, _):
        for q in range(SLOTS):
            @pl.when(n == first_use(q))
            def _(q=q):
                for p, m in ARRIVALS[2:]:
                    if taken_at[p] == first_use(q) and owner_of[p] == q:
                        take_up(p, m)
                for m in range(2):
                    across(q, m).wait_recv()

        a, b = table(core, n, 0), table(core, n, 1)
        weight = jnp.where(table(core, n, 2) == 1, F32(0.5), F32(1.0))
        for m in range(2):
            z[n, m] = lax.dot_general(
                block(a, m), block(b, m), (((1,), (1,)), ((), ())), preferred_element_type=F32
            ) * (scale * math.log2(math.e))

        @pl.when(a == b)
        def _():
            own = lax.broadcasted_iota(jnp.int32, (full, full), 0) == lax.broadcasted_iota(
                jnp.int32, (full, full), 1
            )
            for m in range(2):
                z[n, m] = jnp.where(own, -1e30, z[n, m])

        for m in range(2):
            score = z[n, m]
            right = jnp.max(score, axis=1, keepdims=True)
            down = jnp.max(score, axis=0, keepdims=True)
            right_sum = jnp.sum(jnp.exp2(score - right), axis=1, keepdims=True)
            down_sum = jnp.sum(jnp.exp2(score - down), axis=0, keepdims=True)
            merge(stat.at[a], m, as_row(right), weight * as_row(right_sum))
            merge(stat.at[b], m, down, weight * down_sum)
        return 0

    level = {0: 0}
    for q in range(1, SLOTS):
        level[q] = level[PARENT[q]] + 1
    taken_at, owner_of = {}, {}
    for q in range(1, SLOTS):
        peers = [p for p in range(SLOTS) if level[p] == level[q]]
        head = min(peers, key=lambda p: (first_use(p), p))
        taken_at[q], owner_of[q] = first_use(head), head

    lax.fori_loop(0, STEPS, first_pass, 0)

    def stat_copy(q):
        return remote(
            stat.at[q], stat_in.at[q], stat_send.at[q], stat_recv.at[q], device(OFFSETS[q], core)
        )

    def norm_copy(q):
        return remote(
            norm.at[0], norm.at[q], norm_send.at[q], norm_recv.at[q], device(OFFSETS[q], core, -1)
        )

    for q in range(1, SLOTS):
        stat_copy(q).start()
    both[...] = stat[0]
    for q in range(1, SLOTS):
        stat_copy(q).wait_recv()
        for m in range(2):
            merge(both, m, stat_in[q, 2 * m : 2 * m + 1, :], stat_in[q, 2 * m + 1 : 2 * m + 2, :])
    both_copy = remote(both, both_in, both_send, both_recv, sibling)
    both_copy.start()
    both_copy.wait()
    for m in range(2):
        merge(both, m, both_in[2 * m : 2 * m + 1, :], both_in[2 * m + 1 : 2 * m + 2, :])
    for m in range(2):
        norm[0, m : m + 1, :] = both[2 * m : 2 * m + 1, :] + jnp.log2(both[2 * m + 1 : 2 * m + 2, :])
    for q in range(1, SLOTS):
        norm_copy(q).start()
    for q in range(1, SLOTS):
        norm_copy(q).wait_recv()

    def half_copy(q):
        return remote(
            acc.at[q, other], half_in.at[q], half_send.at[q], half_recv.at[q], sibling
        )

    def part_copy(q):
        return remote(
            acc.at[q, core], part_in.at[q], part_send.at[q], part_recv.at[q], device(edge(q), core)
        )

    def pass_on(q):
        half_copy(q).wait_recv()
        total = acc[q, core] + half_in[q]
        for child in CHILDREN[q]:
            part_copy(child).wait_recv()
            total = total + part_in[child]
        if q:
            acc[q, core] = total
            part_copy(q).start()
        else:
            o_ref[...] = scale * total

    done = {
        q: max(STEPS - 1 - n for core_ in (0, 1) for n in range(STEPS) if q in WORK[core_][n][:2])
        for q in range(SLOTS)
    }

    def second_pass(step, _):
        n = STEPS - 1 - step
        a, b = table(core, n, 0), table(core, n, 1)
        less = table(core, n, 2).astype(F32)
        left = [as_column(norm[a, m : m + 1, :] + less) for m in range(2)]
        top = [norm[b, m : m + 1, :] + less for m in range(2)]
        zt, zs = z[n, 0], z[n, 1]
        by_row = (jnp.exp2(zs - left[1]) - jnp.exp2(zt - left[0])).astype(BF16)
        by_col = (jnp.exp2(zs - top[1]) - jnp.exp2(zt - top[0])).astype(BF16)
        sa, sb = block(a, 1), block(b, 1)
        forward = jnp.dot(by_row, sb, preferred_element_type=F32) + jnp.dot(
            by_col, sb, preferred_element_type=F32
        )
        acc[a] = acc[a] + forward.reshape(2, shard, width)
        dims = (((0,), (0,)), ((), ()))
        backward = lax.dot_general(by_row, sa, dims, preferred_element_type=F32) + lax.dot_general(
            by_col, sa, dims, preferred_element_type=F32
        )
        acc[b] = acc[b] + backward.reshape(2, shard, width)
        for q in reversed(range(SLOTS)):
            @pl.when(step == done[q])
            def _(q=q):
                half_copy(q).start()
        return 0

    lax.fori_loop(0, STEPS, second_pass, 0)
    for q in reversed(range(SLOTS)):
        pass_on(q)

    for q in range(SLOTS):
        for m in range(2):
            if q:
                tree(q, m).wait_send()
            across(q, m).wait_send()
        half_copy(q).wait_send()
        if q:
            stat_copy(q).wait_send()
            norm_copy(q).wait_send()
            part_copy(q).wait_send()


def on_device(teacher, student):
    shard, width = teacher.shape
    full = 2 * shard
    dma = pltpu.SemaphoreType.DMA
    return pl.pallas_call(
        kernel,
        out_shape=jax.ShapeDtypeStruct((shard, width), F32),
        in_specs=[pl.BlockSpec(memory_space=pltpu.VMEM)] * 2,
        out_specs=pl.BlockSpec(memory_space=pltpu.VMEM),
        scratch_shapes=[
            pltpu.VMEM((SLOTS, 2, 2, shard, width), BF16),
            pltpu.VMEM((STEPS, 2, full, full), F32),
            pltpu.VMEM((SLOTS, 2, shard, width), F32),
            pltpu.VMEM((SLOTS, 8, full), F32),
            pltpu.VMEM((SLOTS, 8, full), F32),
            pltpu.VMEM((8, full), F32),
            pltpu.VMEM((8, full), F32),
            pltpu.VMEM((SLOTS, 8, full), F32),
            pltpu.VMEM((SLOTS, shard, width), F32),
            pltpu.VMEM((SLOTS, shard, width), F32),
            dma((SLOTS, 2)), dma((SLOTS, 2)), dma((SLOTS, 2)), dma((SLOTS, 2)),
            dma((SLOTS,)), dma((SLOTS,)), dma, dma,
            dma((SLOTS,)), dma((SLOTS,)), dma((SLOTS,)), dma((SLOTS,)),
            dma((SLOTS,)), dma((SLOTS,)),
        ],
        compiler_params=pltpu.CompilerParams(
            collective_id=0, has_side_effects=True, vmem_limit_bytes=60 * 1024 * 1024
        ),
    )(teacher, student)


def solution(mesh):
    return jax.shard_map(
        on_device,
        mesh=mesh,
        in_specs=(P(("row", "col"), None), P(("row", "col"), None)),
        out_specs=P(("row", "col"), None),
        check_vma=False,
    )
```

```python
import functools
import math

import jax
import jax.numpy as jnp
from jax import lax
from jax.experimental import pallas as pl
from jax.experimental.pallas import tpu as pltpu
from jax.sharding import PartitionSpec as P

F32 = jnp.float32
BF16 = jnp.bfloat16
MESH = pl.DeviceIdType.MESH
SIDE = 4

OFFSETS = (
    (0, 0, 0), (3, 0, 0), (0, 0, 1), (1, 0, 0), (0, 3, 3), (3, 1, 0),
    (1, 0, 1), (0, 2, 3), (3, 2, 0), (3, 1, 3), (1, 0, 2),
)
PARENT = (None, 0, 0, 0, 0, 1, 2, 4, 5, 5, 6)
SLOTS = len(OFFSETS)
CHILDREN = tuple(tuple(q for q in range(SLOTS) if PARENT[q] == p) for p in range(SLOTS))
LEVEL = []
for parent in PARENT:
    LEVEL.append(0 if parent is None else LEVEL[parent] + 1)
LEVELS = tuple(tuple(q for q in range(SLOTS) if LEVEL[q] == level) for level in range(4))

WORK = (
    (
        (2, 1, 0), (4, 3, 2),
        (1, 6, 5), (6, 5, 4), (7, 3, 0),
        (0, 10, 5), (10, 3, 1), (9, 7, 6), (10, 9, 8),
    ),
    (
        (0, 0, 1), (3, 2, 1), (4, 1, 0),
        (5, 4, 3), (2, 7, 5), (7, 6, 5),
        (8, 1, 0), (8, 6, 3), (9, 2, 1),
    ),
)
ITEMS = len(WORK[0])
STEPS = 2 * ITEMS
ROW_PIECES = 1
STUDENT_LATER = False
SUM_PIECES = 2


def minus(a, b):
    return tuple((p - q) % SIDE for p, q in zip(a, b))


def is_half(a, b):
    d = minus(OFFSETS[a], OFFSETS[b])
    return d == minus((0, 0, 0), d)


def check_work():
    found = [
        min(minus(OFFSETS[a], OFFSETS[b]), minus(OFFSETS[b], OFFSETS[a]))
        for work in WORK
        for a, b1, b2 in work
        for b in (b1, b2)
    ]
    assert len(found) == len(set(found)) == (SIDE**3 + 8) // 2


check_work()


def group_of(item, m):
    return max(max(LEVEL[q] for q in item), 1) - 1 + m


def sequence(core):
    steps = [
        (group_of(item, m), m, n) for n, item in enumerate(WORK[core]) for m in range(2)
    ]
    return tuple((m, n) for _, m, n in sorted(steps))


SEQUENCE = (sequence(0), sequence(1))
GROUP_START = tuple(
    min(
        min(s for s, (m, n) in enumerate(SEQUENCE[core]) if group_of(WORK[core][n], m) == g)
        for core in range(2)
    )
    for g in range(4)
)


def packed(item, m, n):
    a, b1, b2 = item
    return (
        a + b1 * 16 + b2 * 256 + int(is_half(a, b1)) * 4096 + int(is_half(a, b2)) * 8192
        + m * 16384 + n * 32768
    )


STEP_CODES = tuple(tuple(packed(WORK[c][n], m, n) for m, n in SEQUENCE[c]) for c in range(2))
ITEM_CODES = tuple(tuple(packed(item, 0, n) for n, item in enumerate(WORK[c])) for c in range(2))


def look_up(codes, core, at):
    value = jnp.int32(0)
    for n, (one, two) in enumerate(zip(*codes)):
        value = jnp.where(at == n, jnp.where(core == 0, jnp.int32(one), jnp.int32(two)), value)
    return value


def field(code, start, bits):
    return (code >> start) & ((1 << bits) - 1)


DONE = tuple(
    max(ITEMS - 1 - n for work in WORK for n, item in enumerate(work) if q in item)
    for q in range(SLOTS)
)
PASS_ON = {
    2: ((9, 0),), 3: ((8, 0),), 4: ((10, 0),), 5: ((9, 1), (7, 0)), 6: ((8, 1),), 7: ((5, 0), (10, 1)),
}
LAST = (
    (4, 0), (3, 0), (6, 0), (7, 1), (5, 1), (6, 1), (1, 0), (2, 0), (4, 1), (3, 1), (1, 1), (2, 1), (0, 0),
    (0, 1),
)
GATED = True


def kernel(
    t_ref, s_ref, o_ref, rows, z, acc, tile, diff, pen, stat, stat_out, stat_in, both, both_in, norm,
    half_in, part_in,
    tree_send, tree_recv, pair_send, pair_recv, stat_send, stat_recv, both_send, both_recv,
    norm_send, norm_recv, half_send, half_recv, part_send, part_recv,
):
    shard, width = t_ref.shape
    full = 2 * shard
    wide = 2 * full
    scale = 1.0 / (0.1 * math.sqrt(width))
    row = lax.axis_index("row")
    col = lax.axis_index("col")
    core = row & 1
    other = 1 - core
    x, y, zz = col & 3, (row >> 1) & 3, ((col >> 2) << 1) + (row >> 3)
    places = {}

    def device(d, sign=1):
        d = tuple((sign * q) % SIDE for q in d)
        if d not in places:
            to = [(p + q) & 3 if q else p for p, q in zip((x, y, zz), d)]
            places[d] = (((to[2] & 1) << 3) + (to[1] << 1) + core, ((to[2] >> 1) << 2) + to[0])
        return places[d]

    sibling = (row ^ 1, col)

    def edge(q):
        return minus(OFFSETS[q], OFFSETS[PARENT[q]])

    partners = set()
    for q in range(1, SLOTS):
        for d in (OFFSETS[q], edge(q)):
            partners.add(d)
            partners.add(minus((0, 0, 0), d))
    partners = sorted(partners)

    barrier = pltpu.get_barrier_semaphore()
    for d in partners:
        pl.semaphore_signal(barrier, inc=1, device_id=device(d), device_id_type=MESH)
    pl.semaphore_signal(barrier, inc=1, device_id=sibling, device_id_type=MESH)
    rows[0, 0, core] = t_ref[...]
    rows[0, 1, core] = s_ref[...]

    def remote(src, dst, send, recv, to):
        return pltpu.make_async_remote_copy(
            src_ref=src, dst_ref=dst, send_sem=send, recv_sem=recv, device_id=to, device_id_type=MESH
        )

    def piece(q, m, c):
        size = shard // ROW_PIECES
        return rows.at[q, m, core, pl.ds(c * size, size)]

    def tree(q, m, c):
        return remote(
            piece(PARENT[q], m, c), piece(q, m, c), tree_send.at[q, m, c], tree_recv.at[q, m, c],
            device(edge(q), -1),
        )

    def across(q, m, c):
        return remote(
            piece(q, m, c), piece(q, m, c), pair_send.at[q, m, c], pair_recv.at[q, m, c], sibling
        )

    def take_up(level, m):
        for c in range(ROW_PIECES):
            for q in LEVELS[level]:
                if q:
                    tree(q, m, c).wait_recv()
                for child in CHILDREN[q]:
                    tree(child, m, c).start()
                across(q, m, c).start()

    def arrive(level, m):
        for c in range(ROW_PIECES):
            for q in LEVELS[level]:
                across(q, m, c).wait_recv()

    def open_group(g):
        if g + 1 < len(LEVELS):
            take_up(g + 1, 0)
        if g or STUDENT_LATER:
            take_up(g, 1)
        if g == 0:
            arrive(0, 0)
        if g == 1:
            arrive(0, 1)
        if g + 1 < len(LEVELS):
            arrive(g + 1, 0)
        if g:
            arrive(g, 1)

    acc[...] = jnp.zeros_like(acc)
    for m in range(2):
        stat[:, m, 0:1, :] = jnp.full((SLOTS, 1, full), -1e30, F32)
        stat[:, m, 1:2, :] = jnp.zeros((SLOTS, 1, full), F32)
    pen[...] = jnp.where(
        lax.broadcasted_iota(jnp.int32, (128, 128), 0) == lax.broadcasted_iota(jnp.int32, (128, 128), 1),
        F32(-1e30), F32(0.0),
    )
    pl.semaphore_wait(barrier, len(partners) + 1)
    take_up(0, 0)
    if not STUDENT_LATER:
        take_up(0, 1)

    def block(q, m):
        return rows[q, m].reshape(full, width)

    def two(b1, b2, m):
        return jnp.concatenate([block(b1, m), block(b2, m)], axis=0)

    def ends(code):
        return field(code, 0, 4), field(code, 4, 4), field(code, 8, 4)

    def scores(code, par):
        a, b1, b2 = ends(code)
        m = field(code, 14, 1)
        less = [jnp.full((1, full), field(code, bit, 1).astype(F32)) for bit in (12, 13)]
        tile[par] = lax.dot_general(
            block(a, m), two(b1, b2, m), (((1,), (1,)), ((), ())), preferred_element_type=F32
        ) * (scale * math.log2(math.e)) - jnp.concatenate(less, axis=1)
        own = (a == b1).astype(F32)
        for k in range(0, full, 128):
            tile[par, k : k + 128, k : k + 128] += pen[...] * own

    def merge(ref, top, total):
        old = ref[0:1, :]
        new = jnp.maximum(old, top)
        ref[1:2, :] = ref[1:2, :] * jnp.exp2(old - new) + total * jnp.exp2(top - new)
        ref[0:1, :] = new

    def lanes(value):
        return [value[:, j : j + 128] for j in range(0, wide, 128)]

    def statistics(code, par):
        a, b1, b2 = ends(code)
        m = field(code, 14, 1)
        at = m * ITEMS + field(code, 15, 4)
        right, down = [], None
        for k in range(0, full, 128):
            score = tile[par, k : k + 128, :]
            z[at, k : k + 128, :] = score
            most = functools.reduce(jnp.maximum, lanes(score))
            right.append(jnp.max(jnp.transpose(most), axis=0, keepdims=True))
            most = jnp.max(score.reshape(16, 8, wide), axis=0)
            down = most if down is None else jnp.maximum(down, most)
        down = jnp.max(down, axis=0, keepdims=True)
        right = jnp.concatenate(right, axis=1)
        column = jnp.transpose(jnp.broadcast_to(right, (128, full)))
        right_sum, down_sum = [], None
        for k in range(0, full, 128):
            score = tile[par, k : k + 128, :]
            across_ = sum(jnp.exp2(part - column[k : k + 128]) for part in lanes(score))
            right_sum.append(jnp.sum(jnp.transpose(across_), axis=0, keepdims=True))
            below = jnp.sum(jnp.exp2(score - down).reshape(16, 8, wide), axis=0)
            down_sum = below if down_sum is None else down_sum + below
        down_sum = jnp.sum(down_sum, axis=0, keepdims=True)
        merge(stat.at[a, m], right, jnp.concatenate(right_sum, axis=1))
        merge(stat.at[b1, m], down[:, :full], down_sum[:, :full])
        merge(stat.at[b2, m], down[:, full:], down_sum[:, full:])

    open_group(0)
    first = look_up(STEP_CODES, core, 0)
    scores(first, 0)

    def first_pass(h, code):
        for par in range(2):
            for g in range(1, 4):
                if (GROUP_START[g] - 1) % 2 == par:
                    @pl.when(h == (GROUP_START[g] - 1) // 2)
                    def _(g=g):
                        open_group(g)
            later = look_up(STEP_CODES, core, jnp.minimum(2 * h + par + 1, STEPS - 1))
            scores(later, 1 - par)
            statistics(code, par)
            code = later
        return code

    lax.fori_loop(0, STEPS // 2, first_pass, first)

    def stat_copy(q):
        return remote(
            stat_out.at[q], stat_in.at[q], stat_send.at[q], stat_recv.at[q], device(OFFSETS[q])
        )

    def norm_copy(q):
        return remote(
            norm.at[0], norm.at[q], norm_send.at[q], norm_recv.at[q], device(OFFSETS[q], -1)
        )

    for q in range(1, SLOTS):
        for m in range(2):
            stat_out[q, 2 * m : 2 * m + 2, :] = stat[q, m, 0:2, :]
        stat_copy(q).start()
    for q in range(1, SLOTS):
        stat_copy(q).wait_recv()
    for m in range(2):
        tops = [stat[0, m, 0:1, :]] + [stat_in[q, 2 * m : 2 * m + 1, :] for q in range(1, SLOTS)]
        sums = [stat[0, m, 1:2, :]] + [stat_in[q, 2 * m + 1 : 2 * m + 2, :] for q in range(1, SLOTS)]
        top = functools.reduce(jnp.maximum, tops)
        both[2 * m : 2 * m + 1, :] = top
        both[2 * m + 1 : 2 * m + 2, :] = sum(s * jnp.exp2(t - top) for t, s in zip(tops, sums))
    both_copy = remote(both, both_in, both_send, both_recv, sibling)
    both_copy.start()
    both_copy.wait()
    for m in range(2):
        one, two_ = both[2 * m : 2 * m + 1, :], both_in[2 * m : 2 * m + 1, :]
        top = jnp.maximum(one, two_)
        norm[0, m : m + 1, :] = top + jnp.log2(
            both[2 * m + 1 : 2 * m + 2, :] * jnp.exp2(one - top)
            + both_in[2 * m + 1 : 2 * m + 2, :] * jnp.exp2(two_ - top)
        )
    for q in range(1, SLOTS):
        norm_copy(q).start()
    for q in range(1, SLOTS):
        norm_copy(q).wait_recv()

    def half_copy(q):
        return remote(acc.at[q, other], half_in.at[q], half_send.at[q], half_recv.at[q], sibling)

    def part_copy(q, c):
        size = shard // SUM_PIECES
        return remote(
            acc.at[q, core, pl.ds(c * size, size)], part_in.at[q, pl.ds(c * size, size)],
            part_send.at[q, c], part_recv.at[q, c], device(edge(q)),
        )

    def pass_on(q, c):
        if c == 0:
            half_copy(q).wait_recv()
        elif q and GATED:
            part_copy(q, c - 1).wait_send()
        size = shard // SUM_PIECES
        at = pl.ds(c * size, size)
        total = acc[q, core, at] + half_in[q, at]
        for child in CHILDREN[q]:
            part_copy(child, c).wait_recv()
            total = total + part_in[child, at]
        if q:
            acc[q, core, at] = total
            part_copy(q, c).start()
        else:
            o_ref[at] = scale * total

    def column_of(line):
        return jnp.concatenate([jnp.transpose(jnp.broadcast_to(line, (128, full)))] * (wide // 128), axis=1)

    def differences(code, par):
        a, b1, b2 = ends(code)
        n = field(code, 15, 4)
        left = [column_of(norm[a, m : m + 1, :]) for m in range(2)]
        top = [
            jnp.concatenate([norm[b1, m : m + 1, :], norm[b2, m : m + 1, :]], axis=1) for m in range(2)
        ]
        zt, zs = z[n], z[ITEMS + n]
        diff[par, 0] = (jnp.exp2(zs - left[1]) - jnp.exp2(zt - left[0])).astype(BF16)
        diff[par, 1] = (jnp.exp2(zs - top[1]) - jnp.exp2(zt - top[0])).astype(BF16)

    def products(code, par):
        a, b1, b2 = ends(code)
        by_row, by_col = diff[par, 0], diff[par, 1]
        sa, sb = block(a, 1), two(b1, b2, 1)
        forward = jnp.dot(
            jnp.concatenate([by_row, by_col], axis=1), jnp.concatenate([sb, sb], axis=0),
            preferred_element_type=F32,
        )
        acc[a] = acc[a] + forward.reshape(2, shard, width)
        backward = lax.dot_general(
            jnp.concatenate([by_row, by_col], axis=0), jnp.concatenate([sa, sa], axis=0),
            (((0,), (0,)), ((), ())), preferred_element_type=F32,
        )
        acc[b1] = acc[b1] + backward[:full].reshape(2, shard, width)
        acc[b2] = acc[b2] + backward[full:].reshape(2, shard, width)

    def after(step):
        for q in reversed(range(SLOTS)):
            if DONE[q] == step:
                half_copy(q).start()
        for q, c in PASS_ON.get(step, ()):
            pass_on(q, c)

    first = look_up(ITEM_CODES, core, ITEMS - 1)
    differences(first, 0)

    def second_pass(h, code):
        for par in range(2):
            later = look_up(ITEM_CODES, core, ITEMS - 2 - (2 * h + par))
            differences(later, 1 - par)
            products(code, par)
            code = later
            for step in range(par, ITEMS - 1, 2):
                if step in DONE or step in PASS_ON:
                    @pl.when(h == step // 2)
                    def _(step=step):
                        after(step)
        return code

    last = lax.fori_loop(0, (ITEMS - 1) // 2, second_pass, first)
    products(last, 0)
    after(ITEMS - 1)
    for q, c in LAST:
        pass_on(q, c)

    for q in range(SLOTS):
        for m in range(2):
            for c in range(ROW_PIECES):
                if q:
                    tree(q, m, c).wait_send()
                across(q, m, c).wait_send()
        half_copy(q).wait_send()
        if q:
            stat_copy(q).wait_send()
            norm_copy(q).wait_send()
            for c in range(SUM_PIECES - 1 if GATED else 0, SUM_PIECES):
                part_copy(q, c).wait_send()


def on_device(teacher, student):
    shard, width = teacher.shape
    full = 2 * shard
    dma = pltpu.SemaphoreType.DMA
    return pl.pallas_call(
        kernel,
        out_shape=jax.ShapeDtypeStruct((shard, width), F32),
        in_specs=[pl.BlockSpec(memory_space=pltpu.VMEM)] * 2,
        out_specs=pl.BlockSpec(memory_space=pltpu.VMEM),
        scratch_shapes=[
            pltpu.VMEM((SLOTS, 2, 2, shard, width), BF16),
            pltpu.VMEM((STEPS, full, 2 * full), F32),
            pltpu.VMEM((SLOTS, 2, shard, width), F32),
            pltpu.VMEM((2, full, 2 * full), F32),
            pltpu.VMEM((2, 2, full, 2 * full), BF16),
            pltpu.VMEM((128, 128), F32),
            pltpu.VMEM((SLOTS, 2, 8, full), F32),
            pltpu.VMEM((SLOTS, 4, full), F32),
            pltpu.VMEM((SLOTS, 4, full), F32),
            pltpu.VMEM((4, full), F32),
            pltpu.VMEM((4, full), F32),
            pltpu.VMEM((SLOTS, 2, full), F32),
            pltpu.VMEM((SLOTS, shard, width), F32),
            pltpu.VMEM((SLOTS, shard, width), F32),
            dma((SLOTS, 2, ROW_PIECES)), dma((SLOTS, 2, ROW_PIECES)),
            dma((SLOTS, 2, ROW_PIECES)), dma((SLOTS, 2, ROW_PIECES)),
            dma((SLOTS,)), dma((SLOTS,)), dma, dma,
            dma((SLOTS,)), dma((SLOTS,)), dma((SLOTS,)), dma((SLOTS,)),
            dma((SLOTS, SUM_PIECES)), dma((SLOTS, SUM_PIECES)),
        ],
        compiler_params=pltpu.CompilerParams(
            collective_id=0, has_side_effects=True, vmem_limit_bytes=62 * 1024 * 1024
        ),
    )(teacher, student)


def solution(mesh):
    return jax.shard_map(
        on_device,
        mesh=mesh,
        in_specs=(P(("row", "col"), None), P(("row", "col"), None)),
        out_specs=P(("row", "col"), None),
        check_vma=False,
    )
```

```python
import functools
import math

import jax
import jax.numpy as jnp
from jax import lax
from jax.experimental import pallas as pl
from jax.experimental.pallas import tpu as pltpu
from jax.sharding import PartitionSpec as P

F32 = jnp.float32
BF16 = jnp.bfloat16
MESH = pl.DeviceIdType.MESH
SIDE = 4

OFFSETS = (
    (0, 0, 0), (3, 0, 0), (0, 0, 1), (1, 0, 0), (0, 3, 3), (3, 1, 0),
    (1, 0, 1), (0, 2, 3), (3, 2, 0), (3, 1, 3), (1, 0, 2),
)
PARENT = (None, 0, 0, 0, 0, 1, 2, 4, 5, 5, 6)
SLOTS = len(OFFSETS)
CHILDREN = tuple(tuple(q for q in range(SLOTS) if PARENT[q] == p) for p in range(SLOTS))
LEVEL = []
for parent in PARENT:
    LEVEL.append(0 if parent is None else LEVEL[parent] + 1)
LEVELS = tuple(tuple(q for q in range(SLOTS) if LEVEL[q] == level) for level in range(4))

WORK = (
    (
        (2, 1, 0), (4, 3, 2),
        (1, 6, 5), (6, 5, 4), (7, 3, 0),
        (9, 7, 6), (0, 10, 5), (10, 3, 1), (10, 9, 8),
    ),
    (
        (0, 0, 1), (3, 2, 1), (4, 1, 0),
        (5, 4, 3), (2, 7, 5), (7, 6, 5),
        (9, 2, 1), (8, 1, 0), (8, 6, 3),
    ),
)
ITEMS = len(WORK[0])
STEPS = 2 * ITEMS
ROW_PIECES = 1
SUM_PIECES = 2


def minus(a, b):
    return tuple((p - q) % SIDE for p, q in zip(a, b))


def is_half(a, b):
    d = minus(OFFSETS[a], OFFSETS[b])
    return d == minus((0, 0, 0), d)


def check_work():
    found = [
        min(minus(OFFSETS[a], OFFSETS[b]), minus(OFFSETS[b], OFFSETS[a]))
        for work in WORK
        for a, b1, b2 in work
        for b in (b1, b2)
    ]
    assert len(found) == len(set(found)) == (SIDE**3 + 8) // 2


check_work()


def group_of(item, m):
    return max(max(LEVEL[q] for q in item), 1) - 1 + m


def sequence(core):
    steps = [(group_of(item, m), m, n) for n, item in enumerate(WORK[core]) for m in range(2)]
    return tuple((m, n) for _, m, n in sorted(steps))


SEQUENCE = (sequence(0), sequence(1))
GROUP_START = tuple(
    min(
        min(s for s, (m, n) in enumerate(SEQUENCE[core]) if group_of(WORK[core][n], m) == g)
        for core in range(2)
    )
    for g in range(4)
)
TAKEN = {-1: ((0, 0), (0, 1), (1, 0), (1, 1), (2, 0)), 0: ((2, 1), (3, 0)), 6: ((3, 1),)}
HANDED = {-1: ((0, 0), (1, 0)), 0: ((2, 0), (0, 1), (1, 1)), 6: ((3, 0),), 10: ((2, 1),), 12: ((3, 1),)}
assert GROUP_START == (0, 2, 7, 14)


def packed(item, m, n):
    a, b1, b2 = item
    return (
        a + b1 * 16 + b2 * 256 + int(is_half(a, b1)) * 4096 + int(is_half(a, b2)) * 8192
        + m * 16384 + n * 32768
    )


STEP_CODES = tuple(tuple(packed(WORK[c][n], m, n) for m, n in SEQUENCE[c]) for c in range(2))
ITEM_CODES = tuple(tuple(packed(item, 0, n) for n, item in enumerate(WORK[c])) for c in range(2))


def look_up(codes, core, at):
    value = jnp.int32(0)
    for n, (one, two) in enumerate(zip(*codes)):
        value = jnp.where(at == n, jnp.where(core == 0, jnp.int32(one), jnp.int32(two)), value)
    return value


def field(code, start, bits):
    return (code >> start) & ((1 << bits) - 1)


DONE = tuple(
    max(ITEMS - 1 - n for work in WORK for n, item in enumerate(work) if q in item)
    for q in range(SLOTS)
)
GOES_TO = {(q, c): PARENT[q] for q in range(1, SLOTS) for c in range(SUM_PIECES)}
GOES_TO[5, 1] = 0
GOES_TO[6, 0] = 3
PASS_ON = {
    3: ((8, 0), (10, 0)), 4: ((9, 0),), 5: ((8, 1), (10, 1), (7, 0)), 6: ((9, 1),), 7: ((7, 1),),
}
LAST = (
    (6, 0), (4, 0), (3, 1), (5, 0), (1, 1), (2, 0), (6, 1), (4, 1), (5, 1), (3, 0), (1, 0), (2, 1), (0, 0), (0, 1),
)
ORDER = tuple(piece for step in sorted(PASS_ON) for piece in PASS_ON[step]) + LAST
FIRST = tuple(next(piece for piece in ORDER if piece[0] == q) for q in range(SLOTS))
SECOND = tuple(next(piece for piece in ORDER[::-1] if piece[0] == q) for q in range(SLOTS))
assert len(set(ORDER)) == len(ORDER) == SLOTS * SUM_PIECES == 2 * SLOTS


def kernel(
    t_ref, s_ref, o_ref, rows, z, acc, tile, diff, pen, stat, stat_out, stat_in, both, both_in, norm,
    half_in, part_in,
    tree_send, tree_recv, pair_send, pair_recv, stat_send, stat_recv, both_send, both_recv,
    norm_send, norm_recv, half_send, half_recv, part_send, part_recv,
):
    shard, width = t_ref.shape
    full = 2 * shard
    wide = 2 * full
    scale = 1.0 / (0.1 * math.sqrt(width))
    row = lax.axis_index("row")
    col = lax.axis_index("col")
    core = row & 1
    other = 1 - core
    x, y, zz = col & 3, (row >> 1) & 3, ((col >> 2) << 1) + (row >> 3)
    places = {}

    def device(d, sign=1):
        d = tuple((sign * q) % SIDE for q in d)
        if d not in places:
            to = [(p + q) & 3 if q else p for p, q in zip((x, y, zz), d)]
            places[d] = (((to[2] & 1) << 3) + (to[1] << 1) + core, ((to[2] >> 1) << 2) + to[0])
        return places[d]

    sibling = (row ^ 1, col)

    def edge(q):
        return minus(OFFSETS[q], OFFSETS[PARENT[q]])

    def sum_edge(q, c):
        return minus(OFFSETS[q], OFFSETS[GOES_TO[q, c]])

    partners = set()
    for q in range(1, SLOTS):
        for d in [OFFSETS[q], edge(q)] + [sum_edge(q, c) for c in range(SUM_PIECES)]:
            partners.add(d)
            partners.add(minus((0, 0, 0), d))
    partners = sorted(partners)

    barrier = pltpu.get_barrier_semaphore()
    for d in partners:
        pl.semaphore_signal(barrier, inc=1, device_id=device(d), device_id_type=MESH)
    pl.semaphore_signal(barrier, inc=1, device_id=sibling, device_id_type=MESH)
    rows[0, 0, core] = t_ref[...]
    rows[0, 1, core] = s_ref[...]

    def remote(src, dst, send, recv, to):
        return pltpu.make_async_remote_copy(
            src_ref=src, dst_ref=dst, send_sem=send, recv_sem=recv, device_id=to, device_id_type=MESH
        )

    def piece(q, m, c):
        size = shard // ROW_PIECES
        return rows.at[q, m, core, pl.ds(c * size, size)]

    def tree(q, m, c):
        return remote(
            piece(PARENT[q], m, c), piece(q, m, c), tree_send.at[q, m, c], tree_recv.at[q, m, c],
            device(edge(q), -1),
        )

    def across(q, m, c):
        part = piece(q, m, c)
        return remote(part, part, pair_send.at[q, m, c], pair_recv.at[q, m, c], sibling)

    def take_up(level, n):
        m, c = n // ROW_PIECES, n % ROW_PIECES
        if level == 0 and n:
            for child in CHILDREN[0]:
                tree(child, (n - 1) // ROW_PIECES, (n - 1) % ROW_PIECES).wait_send()
        for q in LEVELS[level]:
            if q:
                tree(q, m, c).wait_recv()
            for child in CHILDREN[q]:
                tree(child, m, c).start()
            across(q, m, c).start()

    def arrive(level, m):
        for q in LEVELS[level]:
            for c in range(ROW_PIECES):
                across(q, m, c).wait_recv()

    def before(step):
        for level, n in TAKEN.get(step, ()):
            take_up(level, n)
        for level, m in HANDED.get(step, ()):
            arrive(level, m)

    acc[...] = jnp.zeros_like(acc)
    for m in range(2):
        stat[:, m, 0:1, :] = jnp.full((SLOTS, 1, full), -1e30, F32)
        stat[:, m, 1:2, :] = jnp.zeros((SLOTS, 1, full), F32)
    pen[...] = jnp.where(
        lax.broadcasted_iota(jnp.int32, (128, 128), 0) == lax.broadcasted_iota(jnp.int32, (128, 128), 1),
        F32(-1e30), F32(0.0),
    )
    pl.semaphore_wait(barrier, len(partners) + 1)

    def block(q, m):
        return rows[q, m].reshape(full, width)

    def two(b1, b2, m):
        return jnp.concatenate([block(b1, m), block(b2, m)], axis=0)

    def ends(code):
        return field(code, 0, 4), field(code, 4, 4), field(code, 8, 4)

    def scores(code, par):
        a, b1, b2 = ends(code)
        m = field(code, 14, 1)
        less = [jnp.full((1, full), field(code, bit, 1).astype(F32)) for bit in (12, 13)]
        tile[par] = lax.dot_general(
            block(a, m), two(b1, b2, m), (((1,), (1,)), ((), ())), preferred_element_type=F32
        ) * (scale * math.log2(math.e)) - jnp.concatenate(less, axis=1)
        own = (a == b1).astype(F32)
        for k in range(0, full, 128):
            tile[par, k : k + 128, k : k + 128] += pen[...] * own

    def merge(ref, top, total):
        old = ref[0:1, :]
        new = jnp.maximum(old, top)
        ref[1:2, :] = ref[1:2, :] * jnp.exp2(old - new) + total * jnp.exp2(top - new)
        ref[0:1, :] = new

    def lanes(value):
        return [value[:, j : j + 128] for j in range(0, wide, 128)]

    def statistics(code, par):
        a, b1, b2 = ends(code)
        m = field(code, 14, 1)
        at = m * ITEMS + field(code, 15, 4)
        right, down = [], None
        for k in range(0, full, 128):
            score = tile[par, k : k + 128, :]
            z[at, k : k + 128, :] = score
            most = functools.reduce(jnp.maximum, lanes(score))
            right.append(jnp.max(jnp.transpose(most), axis=0, keepdims=True))
            most = jnp.max(score.reshape(16, 8, wide), axis=0)
            down = most if down is None else jnp.maximum(down, most)
        down = jnp.max(down, axis=0, keepdims=True)
        right = jnp.concatenate(right, axis=1)
        column = jnp.transpose(jnp.broadcast_to(right, (128, full)))
        right_sum, down_sum = [], None
        for k in range(0, full, 128):
            score = tile[par, k : k + 128, :]
            across_ = sum(jnp.exp2(part - column[k : k + 128]) for part in lanes(score))
            right_sum.append(jnp.sum(jnp.transpose(across_), axis=0, keepdims=True))
            below = jnp.sum(jnp.exp2(score - down).reshape(16, 8, wide), axis=0)
            down_sum = below if down_sum is None else down_sum + below
        down_sum = jnp.sum(down_sum, axis=0, keepdims=True)
        merge(stat.at[a, m], right, jnp.concatenate(right_sum, axis=1))
        merge(stat.at[b1, m], down[:, :full], down_sum[:, :full])
        merge(stat.at[b2, m], down[:, full:], down_sum[:, full:])

    before(-1)
    first = look_up(STEP_CODES, core, 0)
    scores(first, 0)

    def first_pass(h, code):
        for step in sorted(set(TAKEN) | set(HANDED)):
            if step >= 0:
                @pl.when(2 * h == step)
                def _(step=step):
                    before(step)
        for par in range(2):
            later = look_up(STEP_CODES, core, jnp.minimum(2 * h + par + 1, STEPS - 1))
            scores(later, 1 - par)
            statistics(code, par)
            code = later
        return code

    lax.fori_loop(0, STEPS // 2, first_pass, first)

    def stat_copy(q):
        return remote(
            stat_out.at[q], stat_in.at[q], stat_send.at[q], stat_recv.at[q], device(OFFSETS[q])
        )

    def norm_copy(q):
        return remote(
            norm.at[0], norm.at[q], norm_send.at[q], norm_recv.at[q], device(OFFSETS[q], -1)
        )

    for q in range(1, SLOTS):
        for m in range(2):
            stat_out[q, 2 * m : 2 * m + 2, :] = stat[q, m, 0:2, :]
        stat_copy(q).start()
    for q in range(1, SLOTS):
        stat_copy(q).wait_recv()
    for m in range(2):
        tops = [stat[0, m, 0:1, :]] + [stat_in[q, 2 * m : 2 * m + 1, :] for q in range(1, SLOTS)]
        sums = [stat[0, m, 1:2, :]] + [stat_in[q, 2 * m + 1 : 2 * m + 2, :] for q in range(1, SLOTS)]
        top = functools.reduce(jnp.maximum, tops)
        both[2 * m : 2 * m + 1, :] = top
        both[2 * m + 1 : 2 * m + 2, :] = sum(s * jnp.exp2(t - top) for t, s in zip(tops, sums))
    both_copy = remote(both, both_in, both_send, both_recv, sibling)
    both_copy.start()
    both_copy.wait()
    for m in range(2):
        one, two_ = both[2 * m : 2 * m + 1, :], both_in[2 * m : 2 * m + 1, :]
        top = jnp.maximum(one, two_)
        norm[0, m : m + 1, :] = top + jnp.log2(
            both[2 * m + 1 : 2 * m + 2, :] * jnp.exp2(one - top)
            + both_in[2 * m + 1 : 2 * m + 2, :] * jnp.exp2(two_ - top)
        )
    for q in range(1, SLOTS):
        norm_copy(q).start()
    for q in range(1, SLOTS):
        norm_copy(q).wait_recv()

    def half_copy(q):
        return remote(acc.at[q, other], half_in.at[q], half_send.at[q], half_recv.at[q], sibling)

    def part_copy(q, c):
        size = shard // SUM_PIECES
        return remote(
            acc.at[q, core, pl.ds(c * size, size)], part_in.at[q, pl.ds(c * size, size)],
            part_send.at[q, c], part_recv.at[q, c], device(sum_edge(q, c)),
        )

    def pass_on(q, c):
        if (q, c) in FIRST:
            half_copy(q).wait_recv()
        elif q:
            part_copy(q, 1 - c).wait_send()
        size = shard // SUM_PIECES
        at = pl.ds(c * size, size)
        total = acc[q, core, at] + half_in[q, at]
        for child in range(1, SLOTS):
            if GOES_TO[child, c] == q:
                part_copy(child, c).wait_recv()
                total = total + part_in[child, at]
        if q:
            acc[q, core, at] = total
            part_copy(q, c).start()
        else:
            o_ref[at] = scale * total

    def column_of(line):
        return jnp.concatenate([jnp.transpose(jnp.broadcast_to(line, (128, full)))] * (wide // 128), axis=1)

    def differences(code, par):
        a, b1, b2 = ends(code)
        n = field(code, 15, 4)
        left = [column_of(norm[a, m : m + 1, :]) for m in range(2)]
        top = [
            jnp.concatenate([norm[b1, m : m + 1, :], norm[b2, m : m + 1, :]], axis=1) for m in range(2)
        ]
        zt, zs = z[n], z[ITEMS + n]
        diff[par, 0] = (jnp.exp2(zs - left[1]) - jnp.exp2(zt - left[0])).astype(BF16)
        diff[par, 1] = (jnp.exp2(zs - top[1]) - jnp.exp2(zt - top[0])).astype(BF16)

    def products(code, par):
        a, b1, b2 = ends(code)
        by_row, by_col = diff[par, 0], diff[par, 1]
        sa, sb = block(a, 1), two(b1, b2, 1)
        forward = jnp.dot(
            jnp.concatenate([by_row, by_col], axis=1), jnp.concatenate([sb, sb], axis=0),
            preferred_element_type=F32,
        )
        acc[a] = acc[a] + forward.reshape(2, shard, width)
        backward = lax.dot_general(
            jnp.concatenate([by_row, by_col], axis=0), jnp.concatenate([sa, sa], axis=0),
            (((0,), (0,)), ((), ())), preferred_element_type=F32,
        )
        acc[b1] = acc[b1] + backward[:full].reshape(2, shard, width)
        acc[b2] = acc[b2] + backward[full:].reshape(2, shard, width)

    def after(step):
        for q in reversed(range(SLOTS)):
            if DONE[q] == step:
                half_copy(q).start()
        for q, c in PASS_ON.get(step, ()):
            pass_on(q, c)

    first = look_up(ITEM_CODES, core, ITEMS - 1)
    differences(first, 0)

    def second_pass(h, code):
        for par in range(2):
            later = look_up(ITEM_CODES, core, ITEMS - 2 - (2 * h + par))
            differences(later, 1 - par)
            products(code, par)
            code = later
            for step in range(par, ITEMS - 1, 2):
                if step in DONE or step in PASS_ON:
                    @pl.when(h == step // 2)
                    def _(step=step):
                        after(step)
        return code

    last = lax.fori_loop(0, (ITEMS - 1) // 2, second_pass, first)
    products(last, 0)
    after(ITEMS - 1)
    for q, c in LAST:
        pass_on(q, c)

    for q in range(SLOTS):
        for m in range(2):
            for c in range(ROW_PIECES):
                if q and (PARENT[q] or m == 1 and c == ROW_PIECES - 1):
                    tree(q, m, c).wait_send()
                across(q, m, c).wait_send()
        half_copy(q).wait_send()
        if q:
            stat_copy(q).wait_send()
            norm_copy(q).wait_send()
            part_copy(*SECOND[q]).wait_send()


def on_device(teacher, student):
    shard, width = teacher.shape
    full = 2 * shard
    dma = pltpu.SemaphoreType.DMA
    return pl.pallas_call(
        kernel,
        out_shape=jax.ShapeDtypeStruct((shard, width), F32),
        in_specs=[pl.BlockSpec(memory_space=pltpu.VMEM)] * 2,
        out_specs=pl.BlockSpec(memory_space=pltpu.VMEM),
        scratch_shapes=[
            pltpu.VMEM((SLOTS, 2, 2, shard, width), BF16),
            pltpu.VMEM((STEPS, full, 2 * full), F32),
            pltpu.VMEM((SLOTS, 2, shard, width), F32),
            pltpu.VMEM((2, full, 2 * full), F32),
            pltpu.VMEM((2, 2, full, 2 * full), BF16),
            pltpu.VMEM((128, 128), F32),
            pltpu.VMEM((SLOTS, 2, 8, full), F32),
            pltpu.VMEM((SLOTS, 4, full), F32),
            pltpu.VMEM((SLOTS, 4, full), F32),
            pltpu.VMEM((4, full), F32),
            pltpu.VMEM((4, full), F32),
            pltpu.VMEM((SLOTS, 2, full), F32),
            pltpu.VMEM((SLOTS, shard, width), F32),
            pltpu.VMEM((SLOTS, shard, width), F32),
            dma((SLOTS, 2, ROW_PIECES)), dma((SLOTS, 2, ROW_PIECES)),
            dma((SLOTS, 2, ROW_PIECES)), dma((SLOTS, 2, ROW_PIECES)),
            dma((SLOTS,)), dma((SLOTS,)), dma, dma,
            dma((SLOTS,)), dma((SLOTS,)), dma((SLOTS,)), dma((SLOTS,)),
            dma((SLOTS, SUM_PIECES)), dma((SLOTS, SUM_PIECES)),
        ],
        compiler_params=pltpu.CompilerParams(
            collective_id=0, has_side_effects=True, vmem_limit_bytes=62 * 1024 * 1024
        ),
    )(teacher, student)


def solution(mesh):
    return jax.shard_map(
        on_device,
        mesh=mesh,
        in_specs=(P(("row", "col"), None), P(("row", "col"), None)),
        out_specs=P(("row", "col"), None),
        check_vma=False,
    )
```

```python
import functools
import math

import jax
import jax.numpy as jnp
from jax import lax
from jax.experimental import pallas as pl
from jax.experimental.pallas import tpu as pltpu
from jax.sharding import PartitionSpec as P

F32 = jnp.float32
BF16 = jnp.bfloat16
MESH = pl.DeviceIdType.MESH
SIDE = 4

OFFSETS = (
    (0, 0, 0), (3, 0, 0), (0, 0, 1), (1, 0, 0), (0, 3, 3), (3, 1, 0),
    (1, 0, 1), (0, 2, 3), (3, 2, 0), (3, 1, 3), (1, 0, 2),
)
PARENT = (None, 0, 0, 0, 0, 1, 2, 4, 5, 5, 6)
SLOTS = len(OFFSETS)
CHILDREN = tuple(tuple(q for q in range(SLOTS) if PARENT[q] == p) for p in range(SLOTS))
LEVEL = []
for parent in PARENT:
    LEVEL.append(0 if parent is None else LEVEL[parent] + 1)
LEVELS = tuple(tuple(q for q in range(SLOTS) if LEVEL[q] == level) for level in range(4))

WORK = (
    (
        (2, 1, 0), (4, 3, 2),
        (1, 6, 5), (6, 5, 4), (7, 3, 0),
        (9, 7, 6), (0, 10, 5), (10, 3, 1), (10, 9, 8),
    ),
    (
        (0, 0, 1), (3, 2, 1), (4, 1, 0),
        (5, 4, 3), (2, 7, 5), (7, 6, 5),
        (9, 2, 1), (8, 1, 0), (8, 6, 3),
    ),
)
ITEMS = len(WORK[0])
STEPS = 2 * ITEMS
ROW_PIECES = 1
SUM_PIECES = 2


def minus(a, b):
    return tuple((p - q) % SIDE for p, q in zip(a, b))


def is_half(a, b):
    d = minus(OFFSETS[a], OFFSETS[b])
    return d == minus((0, 0, 0), d)


def check_work():
    found = [
        min(minus(OFFSETS[a], OFFSETS[b]), minus(OFFSETS[b], OFFSETS[a]))
        for work in WORK
        for a, b1, b2 in work
        for b in (b1, b2)
    ]
    assert len(found) == len(set(found)) == (SIDE**3 + 8) // 2


check_work()


def group_of(item, m):
    return max(max(LEVEL[q] for q in item), 1) - 1 + m


def sequence(core):
    steps = [(group_of(item, m), m, n) for n, item in enumerate(WORK[core]) for m in range(2)]
    return tuple((m, n) for _, m, n in sorted(steps))


SEQUENCE = (sequence(0), sequence(1))
GROUP_START = tuple(
    min(
        min(s for s, (m, n) in enumerate(SEQUENCE[core]) if group_of(WORK[core][n], m) == g)
        for core in range(2)
    )
    for g in range(4)
)
TAKEN = {-1: ((0, 0), (0, 1), (1, 0), (1, 1), (2, 0)), 1: ((2, 1), (3, 0)), 9: ((3, 1),)}
HANDED = {-1: ((0, 0), (1, 0)), 1: ((2, 0), (0, 1), (1, 1)), 5: ((3, 0),), 9: ((2, 1),), 13: ((3, 1),)}
assert GROUP_START == (0, 2, 7, 14)


def packed(item, m, n):
    a, b1, b2 = item
    return (
        a + b1 * 16 + b2 * 256 + int(is_half(a, b1)) * 4096 + int(is_half(a, b2)) * 8192
        + m * 16384 + n * 32768
    )


STEP_CODES = tuple(tuple(packed(WORK[c][n], m, n) for m, n in SEQUENCE[c]) for c in range(2))
ITEM_CODES = tuple(tuple(packed(item, 0, n) for n, item in enumerate(WORK[c])) for c in range(2))


def look_up(codes, core, at):
    value = jnp.int32(0)
    for n, (one, two) in enumerate(zip(*codes)):
        value = jnp.where(at == n, jnp.where(core == 0, jnp.int32(one), jnp.int32(two)), value)
    return value


def field(code, start, bits):
    return (code >> start) & ((1 << bits) - 1)


FAR_FIRST = tuple(sorted(range(1, SLOTS), key=lambda q: -sum(min(d, SIDE - d) for d in OFFSETS[q])))

DONE = tuple(
    max(ITEMS - 1 - n for work in WORK for n, item in enumerate(work) if q in item)
    for q in range(SLOTS)
)
GOES_TO = {(q, c): PARENT[q] for q in range(1, SLOTS) for c in range(SUM_PIECES)}
GOES_TO[5, 1] = 0
GOES_TO[6, 0] = 3
PASS_ON = {
    3: ((8, 0), (10, 0)), 4: ((9, 0),), 5: ((8, 1), (10, 1), (7, 0)), 6: ((9, 1),), 7: ((7, 1),),
}
LAST = (
    (6, 0), (4, 0), (3, 1), (5, 0), (1, 1), (2, 0), (6, 1), (4, 1), (5, 1), (3, 0), (1, 0), (2, 1), (0, 0), (0, 1),
)
OWN_HALF_AFTER = (2, 0)
ORDER = tuple(piece for step in sorted(PASS_ON) for piece in PASS_ON[step]) + LAST
FIRST = tuple(next(piece for piece in ORDER if piece[0] == q) for q in range(SLOTS))
SECOND = tuple(next(piece for piece in ORDER[::-1] if piece[0] == q) for q in range(SLOTS))
assert len(set(ORDER)) == len(ORDER) == SLOTS * SUM_PIECES == 2 * SLOTS


def kernel(
    t_ref, s_ref, o_ref, rows, z, acc, tile, diff, pen, stat, stat_out, stat_in, both, both_in, norm,
    half_in, part_in,
    tree_send, tree_recv, pair_send, pair_recv, stat_send, stat_recv, both_send, both_recv,
    norm_send, norm_recv, half_send, half_recv, part_send, part_recv,
):
    shard, width = t_ref.shape
    full = 2 * shard
    wide = 2 * full
    scale = 1.0 / (0.1 * math.sqrt(width))
    row = lax.axis_index("row")
    col = lax.axis_index("col")
    core = row & 1
    other = 1 - core
    x, y, zz = col & 3, (row >> 1) & 3, ((col >> 2) << 1) + (row >> 3)
    places = {}

    def device(d, sign=1):
        d = tuple((sign * q) % SIDE for q in d)
        if d not in places:
            to = [(p + q) & 3 if q else p for p, q in zip((x, y, zz), d)]
            places[d] = (((to[2] & 1) << 3) + (to[1] << 1) + core, ((to[2] >> 1) << 2) + to[0])
        return places[d]

    sibling = (row ^ 1, col)

    def edge(q):
        return minus(OFFSETS[q], OFFSETS[PARENT[q]])

    def sum_edge(q, c):
        return minus(OFFSETS[q], OFFSETS[GOES_TO[q, c]])

    partners = set()
    for q in range(1, SLOTS):
        for d in [OFFSETS[q], edge(q)] + [sum_edge(q, c) for c in range(SUM_PIECES)]:
            partners.add(d)
            partners.add(minus((0, 0, 0), d))
    partners = sorted(partners)

    barrier = pltpu.get_barrier_semaphore()
    for d in partners:
        pl.semaphore_signal(barrier, inc=1, device_id=device(d), device_id_type=MESH)
    pl.semaphore_signal(barrier, inc=1, device_id=sibling, device_id_type=MESH)
    rows[0, 0, core] = t_ref[...]
    rows[0, 1, core] = s_ref[...]

    def remote(src, dst, send, recv, to):
        return pltpu.make_async_remote_copy(
            src_ref=src, dst_ref=dst, send_sem=send, recv_sem=recv, device_id=to, device_id_type=MESH
        )

    def piece(q, m, c):
        size = shard // ROW_PIECES
        return rows.at[q, m, core, pl.ds(c * size, size)]

    def tree(q, m, c):
        return remote(
            piece(PARENT[q], m, c), piece(q, m, c), tree_send.at[q, m, c], tree_recv.at[q, m, c],
            device(edge(q), -1),
        )

    def across(q, m, c):
        part = piece(q, m, c)
        return remote(part, part, pair_send.at[q, m, c], pair_recv.at[q, m, c], sibling)

    def take_up(level, n):
        m, c = n // ROW_PIECES, n % ROW_PIECES
        if level == 0 and n:
            for child in CHILDREN[0]:
                tree(child, (n - 1) // ROW_PIECES, (n - 1) % ROW_PIECES).wait_send()
        for q in LEVELS[level]:
            if q:
                tree(q, m, c).wait_recv()
            for child in CHILDREN[q]:
                tree(child, m, c).start()
            across(q, m, c).start()

    def arrive(level, m):
        for q in LEVELS[level]:
            for c in range(ROW_PIECES):
                across(q, m, c).wait_recv()

    def before(step):
        for level, n in TAKEN.get(step, ()):
            take_up(level, n)
        for level, m in HANDED.get(step, ()):
            arrive(level, m)

    acc[...] = jnp.zeros_like(acc)
    for m in range(2):
        stat[:, m, 0:1, :] = jnp.full((SLOTS, 1, full), -1e30, F32)
        stat[:, m, 1:2, :] = jnp.zeros((SLOTS, 1, full), F32)
    pen[...] = jnp.where(
        lax.broadcasted_iota(jnp.int32, (128, 128), 0) == lax.broadcasted_iota(jnp.int32, (128, 128), 1),
        F32(-1e30), F32(0.0),
    )
    pl.semaphore_wait(barrier, len(partners) + 1)

    def block(q, m):
        return rows[q, m].reshape(full, width)

    def two(b1, b2, m):
        return jnp.concatenate([block(b1, m), block(b2, m)], axis=0)

    def ends(code):
        return field(code, 0, 4), field(code, 4, 4), field(code, 8, 4)

    def scores(code, par):
        a, b1, b2 = ends(code)
        m = field(code, 14, 1)
        less = [jnp.full((1, full), field(code, bit, 1).astype(F32)) for bit in (12, 13)]
        tile[par] = lax.dot_general(
            block(a, m), two(b1, b2, m), (((1,), (1,)), ((), ())), preferred_element_type=F32
        ) * (scale * math.log2(math.e)) - jnp.concatenate(less, axis=1)
        own = (a == b1).astype(F32)
        for k in range(0, full, 128):
            tile[par, k : k + 128, k : k + 128] += pen[...] * own

    def merge(ref, top, total):
        old = ref[0:1, :]
        new = jnp.maximum(old, top)
        ref[1:2, :] = ref[1:2, :] * jnp.exp2(old - new) + total * jnp.exp2(top - new)
        ref[0:1, :] = new

    def lanes(value):
        return [value[:, j : j + 128] for j in range(0, wide, 128)]

    def statistics(code, par):
        a, b1, b2 = ends(code)
        m = field(code, 14, 1)
        at = m * ITEMS + field(code, 15, 4)
        right, down = [], None
        for k in range(0, full, 128):
            score = tile[par, k : k + 128, :]
            z[at, k : k + 128, :] = score
            most = functools.reduce(jnp.maximum, lanes(score))
            right.append(jnp.max(jnp.transpose(most), axis=0, keepdims=True))
            most = jnp.max(score.reshape(16, 8, wide), axis=0)
            down = most if down is None else jnp.maximum(down, most)
        down = jnp.max(down, axis=0, keepdims=True)
        right = jnp.concatenate(right, axis=1)
        column = jnp.transpose(jnp.broadcast_to(right, (128, full)))
        right_sum, down_sum = [], None
        for k in range(0, full, 128):
            score = tile[par, k : k + 128, :]
            across_ = sum(jnp.exp2(part - column[k : k + 128]) for part in lanes(score))
            right_sum.append(jnp.sum(jnp.transpose(across_), axis=0, keepdims=True))
            below = jnp.sum(jnp.exp2(score - down).reshape(16, 8, wide), axis=0)
            down_sum = below if down_sum is None else down_sum + below
        down_sum = jnp.sum(down_sum, axis=0, keepdims=True)
        merge(stat.at[a, m], right, jnp.concatenate(right_sum, axis=1))
        merge(stat.at[b1, m], down[:, :full], down_sum[:, :full])
        merge(stat.at[b2, m], down[:, full:], down_sum[:, full:])

    before(-1)
    first, second = look_up(STEP_CODES, core, 0), look_up(STEP_CODES, core, 1)
    scores(first, 0)
    scores(second, 1)
    statistics(first, 0)

    def first_pass(h, code):
        for step in sorted(set(TAKEN) | set(HANDED)):
            if step >= 0:
                @pl.when(2 * h + 1 == step)
                def _(step=step):
                    before(step)
        for par in (1, 0):
            later = look_up(STEP_CODES, core, 2 * h + 3 - par)
            scores(later, 1 - par)
            statistics(code, par)
            code = later
        return code

    statistics(lax.fori_loop(0, STEPS // 2 - 1, first_pass, second), 1)

    def stat_copy(q):
        return remote(
            stat_out.at[q], stat_in.at[q], stat_send.at[q], stat_recv.at[q], device(OFFSETS[q])
        )

    def norm_copy(q):
        return remote(
            norm.at[0], norm.at[q], norm_send.at[q], norm_recv.at[q], device(OFFSETS[q], -1)
        )

    for q in FAR_FIRST:
        for m in range(2):
            stat_out[q, 2 * m : 2 * m + 2, :] = stat[q, m, 0:2, :]
        stat_copy(q).start()
    for q in range(1, SLOTS):
        stat_copy(q).wait_recv()
    for m in range(2):
        tops = [stat[0, m, 0:1, :]] + [stat_in[q, 2 * m : 2 * m + 1, :] for q in range(1, SLOTS)]
        sums = [stat[0, m, 1:2, :]] + [stat_in[q, 2 * m + 1 : 2 * m + 2, :] for q in range(1, SLOTS)]
        top = functools.reduce(jnp.maximum, tops)
        both[2 * m : 2 * m + 1, :] = top
        both[2 * m + 1 : 2 * m + 2, :] = sum(s * jnp.exp2(t - top) for t, s in zip(tops, sums))
    both_copy = remote(both, both_in, both_send, both_recv, sibling)
    both_copy.start()
    both_copy.wait()
    for m in range(2):
        one, two_ = both[2 * m : 2 * m + 1, :], both_in[2 * m : 2 * m + 1, :]
        top = jnp.maximum(one, two_)
        norm[0, m : m + 1, :] = top + jnp.log2(
            both[2 * m + 1 : 2 * m + 2, :] * jnp.exp2(one - top)
            + both_in[2 * m + 1 : 2 * m + 2, :] * jnp.exp2(two_ - top)
        )
    for q in FAR_FIRST:
        norm_copy(q).start()
    for q in range(1, SLOTS):
        norm_copy(q).wait_recv()

    def half_copy(q):
        return remote(acc.at[q, other], half_in.at[q], half_send.at[q], half_recv.at[q], sibling)

    def part_copy(q, c):
        size = shard // SUM_PIECES
        return remote(
            acc.at[q, core, pl.ds(c * size, size)], part_in.at[q, pl.ds(c * size, size)],
            part_send.at[q, c], part_recv.at[q, c], device(sum_edge(q, c)),
        )

    def pass_on(q, c):
        if (q, c) in FIRST:
            half_copy(q).wait_recv()
        elif q:
            part_copy(q, 1 - c).wait_send()
        size = shard // SUM_PIECES
        at = pl.ds(c * size, size)
        total = acc[q, core, at] + half_in[q, at]
        for child in range(1, SLOTS):
            if GOES_TO[child, c] == q:
                part_copy(child, c).wait_recv()
                total = total + part_in[child, at]
        if q:
            acc[q, core, at] = total
            part_copy(q, c).start()
        else:
            o_ref[at] = scale * total

    def column_of(line):
        return jnp.concatenate([jnp.transpose(jnp.broadcast_to(line, (128, full)))] * (wide // 128), axis=1)

    def differences(code, par):
        a, b1, b2 = ends(code)
        n = field(code, 15, 4)
        left = [column_of(norm[a, m : m + 1, :]) for m in range(2)]
        top = [
            jnp.concatenate([norm[b1, m : m + 1, :], norm[b2, m : m + 1, :]], axis=1) for m in range(2)
        ]
        zt, zs = z[n], z[ITEMS + n]
        diff[par, 0] = (jnp.exp2(zs - left[1]) - jnp.exp2(zt - left[0])).astype(BF16)
        diff[par, 1] = (jnp.exp2(zs - top[1]) - jnp.exp2(zt - top[0])).astype(BF16)

    def products(code, par):
        a, b1, b2 = ends(code)
        by_row, by_col = diff[par, 0], diff[par, 1]
        sa, sb = block(a, 1), two(b1, b2, 1)
        forward = jnp.dot(
            jnp.concatenate([by_row, by_col], axis=1), jnp.concatenate([sb, sb], axis=0),
            preferred_element_type=F32,
        )
        acc[a] = acc[a] + forward.reshape(2, shard, width)
        backward = lax.dot_general(
            jnp.concatenate([by_row, by_col], axis=0), jnp.concatenate([sa, sa], axis=0),
            (((0,), (0,)), ((), ())), preferred_element_type=F32,
        )
        acc[b1] = acc[b1] + backward[:full].reshape(2, shard, width)
        acc[b2] = acc[b2] + backward[full:].reshape(2, shard, width)

    def after(step):
        for q in reversed(range(SLOTS)):
            if q and DONE[q] == step:
                half_copy(q).start()
        for q, c in PASS_ON.get(step, ()):
            pass_on(q, c)

    first = look_up(ITEM_CODES, core, ITEMS - 1)
    differences(first, 0)

    def second_pass(h, code):
        for par in range(2):
            later = look_up(ITEM_CODES, core, ITEMS - 2 - (2 * h + par))
            differences(later, 1 - par)
            products(code, par)
            code = later
            for step in range(par, ITEMS - 1, 2):
                if step in DONE or step in PASS_ON:
                    @pl.when(h == step // 2)
                    def _(step=step):
                        after(step)
        return code

    last = lax.fori_loop(0, (ITEMS - 1) // 2, second_pass, first)
    products(last, 0)
    after(ITEMS - 1)
    for q, c in LAST:
        pass_on(q, c)
        if (q, c) == OWN_HALF_AFTER:
            half_copy(0).start()

    for q in range(SLOTS):
        for m in range(2):
            for c in range(ROW_PIECES):
                if q and (PARENT[q] or m == 1 and c == ROW_PIECES - 1):
                    tree(q, m, c).wait_send()
                across(q, m, c).wait_send()
        half_copy(q).wait_send()
        if q:
            stat_copy(q).wait_send()
            norm_copy(q).wait_send()
            part_copy(*SECOND[q]).wait_send()


def on_device(teacher, student):
    shard, width = teacher.shape
    full = 2 * shard
    dma = pltpu.SemaphoreType.DMA
    return pl.pallas_call(
        kernel,
        out_shape=jax.ShapeDtypeStruct((shard, width), F32),
        in_specs=[pl.BlockSpec(memory_space=pltpu.VMEM)] * 2,
        out_specs=pl.BlockSpec(memory_space=pltpu.VMEM),
        scratch_shapes=[
            pltpu.VMEM((SLOTS, 2, 2, shard, width), BF16),
            pltpu.VMEM((STEPS, full, 2 * full), F32),
            pltpu.VMEM((SLOTS, 2, shard, width), F32),
            pltpu.VMEM((2, full, 2 * full), F32),
            pltpu.VMEM((2, 2, full, 2 * full), BF16),
            pltpu.VMEM((128, 128), F32),
            pltpu.VMEM((SLOTS, 2, 8, full), F32),
            pltpu.VMEM((SLOTS, 4, full), F32),
            pltpu.VMEM((SLOTS, 4, full), F32),
            pltpu.VMEM((4, full), F32),
            pltpu.VMEM((4, full), F32),
            pltpu.VMEM((SLOTS, 2, full), F32),
            pltpu.VMEM((SLOTS, shard, width), F32),
            pltpu.VMEM((SLOTS, shard, width), F32),
            dma((SLOTS, 2, ROW_PIECES)), dma((SLOTS, 2, ROW_PIECES)),
            dma((SLOTS, 2, ROW_PIECES)), dma((SLOTS, 2, ROW_PIECES)),
            dma((SLOTS,)), dma((SLOTS,)), dma, dma,
            dma((SLOTS,)), dma((SLOTS,)), dma((SLOTS,)), dma((SLOTS,)),
            dma((SLOTS, SUM_PIECES)), dma((SLOTS, SUM_PIECES)),
        ],
        compiler_params=pltpu.CompilerParams(
            collective_id=0, has_side_effects=True, vmem_limit_bytes=62 * 1024 * 1024
        ),
    )(teacher, student)


def solution(mesh):
    return jax.shard_map(
        on_device,
        mesh=mesh,
        in_specs=(P(("row", "col"), None), P(("row", "col"), None)),
        out_specs=P(("row", "col"), None),
        check_vma=False,
    )
```

```python
import functools
import math

import jax
import jax.numpy as jnp
from jax import lax
from jax.experimental import pallas as pl
from jax.experimental.pallas import tpu as pltpu
from jax.sharding import PartitionSpec as P

F32 = jnp.float32
BF16 = jnp.bfloat16
MESH = pl.DeviceIdType.MESH
SIDE = 4

OFFSETS = (
    (0, 0, 0), (3, 0, 0), (0, 0, 1), (1, 0, 0), (0, 3, 3), (3, 1, 0),
    (1, 0, 1), (0, 2, 3), (3, 2, 0), (3, 1, 3), (1, 0, 2),
)
PARENT = (None, 0, 0, 0, 0, 1, 2, 4, 5, 5, 6)
SLOTS = len(OFFSETS)
CHILDREN = tuple(tuple(q for q in range(SLOTS) if PARENT[q] == p) for p in range(SLOTS))
LEVEL = []
for parent in PARENT:
    LEVEL.append(0 if parent is None else LEVEL[parent] + 1)
LEVELS = tuple(tuple(q for q in range(SLOTS) if LEVEL[q] == level) for level in range(4))

WORK = (
    (
        (2, 1, 0), (4, 3, 2),
        (1, 6, 5), (6, 5, 4), (7, 3, 0),
        (9, 7, 6), (0, 10, 5), (10, 3, 1), (10, 9, 8),
    ),
    (
        (0, 0, 1), (3, 2, 1), (4, 1, 0),
        (5, 4, 3), (2, 7, 5), (7, 6, 5),
        (9, 2, 1), (8, 1, 0), (8, 6, 3),
    ),
)
ITEMS = len(WORK[0])
STEPS = 2 * ITEMS
ROW_PIECES = 1
SUM_PIECES = 2


def minus(a, b):
    return tuple((p - q) % SIDE for p, q in zip(a, b))


def is_half(a, b):
    d = minus(OFFSETS[a], OFFSETS[b])
    return d == minus((0, 0, 0), d)


def check_work():
    found = [
        min(minus(OFFSETS[a], OFFSETS[b]), minus(OFFSETS[b], OFFSETS[a]))
        for work in WORK
        for a, b1, b2 in work
        for b in (b1, b2)
    ]
    assert len(found) == len(set(found)) == (SIDE**3 + 8) // 2


check_work()


def group_of(item, m):
    return max(max(LEVEL[q] for q in item), 1) - 1 + m


def sequence(core):
    steps = [(group_of(item, m), m, n) for n, item in enumerate(WORK[core]) for m in range(2)]
    return tuple((m, n) for _, m, n in sorted(steps))


SEQUENCE = (sequence(0), sequence(1))
GROUP_START = tuple(
    min(
        min(s for s, (m, n) in enumerate(SEQUENCE[core]) if group_of(WORK[core][n], m) == g)
        for core in range(2)
    )
    for g in range(4)
)
TAKEN = {-1: ((0, 1), (1, 0), (1, 1), (2, 0)), 1: ((2, 1), (3, 0)), 9: ((3, 1),)}
HANDED = {-1: ((0, 0), (1, 0)), 1: ((2, 0), (0, 1), (1, 1)), 5: ((3, 0),), 9: ((2, 1),), 13: ((3, 1),)}
assert GROUP_START == (0, 2, 7, 14)


def packed(item, m, n):
    a, b1, b2 = item
    return (
        a + b1 * 16 + b2 * 256 + int(is_half(a, b1)) * 4096 + int(is_half(a, b2)) * 8192
        + m * 16384 + n * 32768
    )


STEP_CODES = tuple(tuple(packed(WORK[c][n], m, n) for m, n in SEQUENCE[c]) for c in range(2))
ITEM_CODES = tuple(tuple(packed(item, 0, n) for n, item in enumerate(WORK[c])) for c in range(2))


def look_up(codes, core, at):
    value = jnp.int32(0)
    for n, (one, two) in enumerate(zip(*codes)):
        value = jnp.where(at == n, jnp.where(core == 0, jnp.int32(one), jnp.int32(two)), value)
    return value


def field(code, start, bits):
    return (code >> start) & ((1 << bits) - 1)


FAR_FIRST = tuple(sorted(range(1, SLOTS), key=lambda q: -sum(min(d, SIDE - d) for d in OFFSETS[q])))

DONE = tuple(
    max(ITEMS - 1 - n for work in WORK for n, item in enumerate(work) if q in item)
    for q in range(SLOTS)
)
GOES_TO = {(q, c): PARENT[q] for q in range(1, SLOTS) for c in range(SUM_PIECES)}
GOES_TO[5, 1] = 0
GOES_TO[6, 0] = 3
PASS_ON = {
    3: ((8, 0), (10, 0)), 4: ((9, 0),), 5: ((8, 1), (10, 1), (7, 0)), 6: ((9, 1),), 7: ((7, 1),),
}
LAST = (
    (6, 0), (4, 0), (3, 1), (5, 0), (1, 1), (2, 0), (6, 1), (4, 1), (5, 1), (3, 0), (1, 0), (2, 1), (0, 0), (0, 1),
)
OWN_HALF_AFTER = (2, 0)
ORDER = tuple(piece for step in sorted(PASS_ON) for piece in PASS_ON[step]) + LAST
FIRST = tuple(next(piece for piece in ORDER if piece[0] == q) for q in range(SLOTS))
SECOND = tuple(next(piece for piece in ORDER[::-1] if piece[0] == q) for q in range(SLOTS))
assert len(set(ORDER)) == len(ORDER) == SLOTS * SUM_PIECES == 2 * SLOTS


def kernel(
    t_ref, s_ref, o_ref, rows, z, acc, tile, diff, pen, stat, stat_out, stat_in, both, both_in, norm,
    half_in, part_in,
    tree_send, tree_recv, pair_send, pair_recv, stat_send, stat_recv, both_send, both_recv,
    norm_send, norm_recv, half_send, half_recv, part_send, part_recv,
):
    shard, width = t_ref.shape
    full = 2 * shard
    wide = 2 * full
    scale = 1.0 / (0.1 * math.sqrt(width))
    row = lax.axis_index("row")
    col = lax.axis_index("col")
    core = row & 1
    other = 1 - core
    x, y, zz = col & 3, (row >> 1) & 3, ((col >> 2) << 1) + (row >> 3)
    places = {}

    def device(d, sign=1):
        d = tuple((sign * q) % SIDE for q in d)
        if d not in places:
            to = [(p + q) & 3 if q else p for p, q in zip((x, y, zz), d)]
            places[d] = (((to[2] & 1) << 3) + (to[1] << 1) + core, ((to[2] >> 1) << 2) + to[0])
        return places[d]

    sibling = (row ^ 1, col)

    def edge(q):
        return minus(OFFSETS[q], OFFSETS[PARENT[q]])

    def sum_edge(q, c):
        return minus(OFFSETS[q], OFFSETS[GOES_TO[q, c]])

    partners = set()
    for q in range(1, SLOTS):
        for d in [OFFSETS[q], edge(q)] + [sum_edge(q, c) for c in range(SUM_PIECES)]:
            partners.add(d)
            partners.add(minus((0, 0, 0), d))
    partners = sorted(partners)

    barrier = pltpu.get_barrier_semaphore()
    for d in partners:
        pl.semaphore_signal(barrier, inc=1, device_id=device(d), device_id_type=MESH)
    pl.semaphore_signal(barrier, inc=1, device_id=sibling, device_id_type=MESH)
    rows[0, 0, core] = t_ref[...]
    rows[0, 1, core] = s_ref[...]

    def remote(src, dst, send, recv, to):
        return pltpu.make_async_remote_copy(
            src_ref=src, dst_ref=dst, send_sem=send, recv_sem=recv, device_id=to, device_id_type=MESH
        )

    def piece(q, m, c):
        size = shard // ROW_PIECES
        return rows.at[q, m, core, pl.ds(c * size, size)]

    def tree(q, m, c):
        return remote(
            piece(PARENT[q], m, c), piece(q, m, c), tree_send.at[q, m, c], tree_recv.at[q, m, c],
            device(edge(q), -1),
        )

    def across(q, m, c):
        part = piece(q, m, c)
        return remote(part, part, pair_send.at[q, m, c], pair_recv.at[q, m, c], sibling)

    def take_up(level, n):
        m, c = n // ROW_PIECES, n % ROW_PIECES
        if level == 0 and n:
            for child in CHILDREN[0]:
                tree(child, (n - 1) // ROW_PIECES, (n - 1) % ROW_PIECES).wait_send()
        for q in LEVELS[level]:
            if q:
                tree(q, m, c).wait_recv()
            for child in CHILDREN[q]:
                tree(child, m, c).start()
            across(q, m, c).start()

    def arrive(level, m):
        for q in LEVELS[level]:
            for c in range(ROW_PIECES):
                across(q, m, c).wait_recv()

    def before(step):
        for level, n in TAKEN.get(step, ()):
            take_up(level, n)
        for level, m in HANDED.get(step, ()):
            arrive(level, m)

    pl.semaphore_wait(barrier, len(partners) + 1)
    take_up(0, 0)

    acc[...] = jnp.zeros_like(acc)
    for m in range(2):
        stat[:, m, 0:1, :] = jnp.full((SLOTS, 1, full), -1e30, F32)
        stat[:, m, 1:2, :] = jnp.zeros((SLOTS, 1, full), F32)
    pen[...] = jnp.where(
        lax.broadcasted_iota(jnp.int32, (128, 128), 0) == lax.broadcasted_iota(jnp.int32, (128, 128), 1),
        F32(-1e30), F32(0.0),
    )

    def block(q, m):
        return rows[q, m].reshape(full, width)

    def two(b1, b2, m):
        return jnp.concatenate([block(b1, m), block(b2, m)], axis=0)

    def ends(code):
        return field(code, 0, 4), field(code, 4, 4), field(code, 8, 4)

    def scores(code, par):
        a, b1, b2 = ends(code)
        m = field(code, 14, 1)
        less = [jnp.full((1, full), field(code, bit, 1).astype(F32)) for bit in (12, 13)]
        tile[par] = lax.dot_general(
            block(a, m), two(b1, b2, m), (((1,), (1,)), ((), ())), preferred_element_type=F32
        ) * (scale * math.log2(math.e)) - jnp.concatenate(less, axis=1)
        own = (a == b1).astype(F32)
        for k in range(0, full, 128):
            tile[par, k : k + 128, k : k + 128] += pen[...] * own

    def merge(ref, top, total):
        old = ref[0:1, :]
        new = jnp.maximum(old, top)
        ref[1:2, :] = ref[1:2, :] * jnp.exp2(old - new) + total * jnp.exp2(top - new)
        ref[0:1, :] = new

    def lanes(value):
        return [value[:, j : j + 128] for j in range(0, wide, 128)]

    def statistics(code, par):
        a, b1, b2 = ends(code)
        m = field(code, 14, 1)
        at = m * ITEMS + field(code, 15, 4)
        right, down = [], None
        for k in range(0, full, 128):
            score = tile[par, k : k + 128, :]
            z[at, k : k + 128, :] = score
            most = functools.reduce(jnp.maximum, lanes(score))
            right.append(jnp.max(jnp.transpose(most), axis=0, keepdims=True))
            most = jnp.max(score.reshape(16, 8, wide), axis=0)
            down = most if down is None else jnp.maximum(down, most)
        down = jnp.max(down, axis=0, keepdims=True)
        right = jnp.concatenate(right, axis=1)
        column = jnp.transpose(jnp.broadcast_to(right, (128, full)))
        right_sum, down_sum = [], None
        for k in range(0, full, 128):
            score = tile[par, k : k + 128, :]
            across_ = sum(jnp.exp2(part - column[k : k + 128]) for part in lanes(score))
            right_sum.append(jnp.sum(jnp.transpose(across_), axis=0, keepdims=True))
            below = jnp.sum(jnp.exp2(score - down).reshape(16, 8, wide), axis=0)
            down_sum = below if down_sum is None else down_sum + below
        down_sum = jnp.sum(down_sum, axis=0, keepdims=True)
        merge(stat.at[a, m], right, jnp.concatenate(right_sum, axis=1))
        merge(stat.at[b1, m], down[:, :full], down_sum[:, :full])
        merge(stat.at[b2, m], down[:, full:], down_sum[:, full:])

    before(-1)
    first, second = look_up(STEP_CODES, core, 0), look_up(STEP_CODES, core, 1)
    scores(first, 0)
    scores(second, 1)
    statistics(first, 0)

    def first_pass(h, code):
        for step in sorted(set(TAKEN) | set(HANDED)):
            if step >= 0:
                @pl.when(2 * h + 1 == step)
                def _(step=step):
                    before(step)
        for par in (1, 0):
            later = look_up(STEP_CODES, core, 2 * h + 3 - par)
            scores(later, 1 - par)
            statistics(code, par)
            code = later
        return code

    statistics(lax.fori_loop(0, STEPS // 2 - 1, first_pass, second), 1)

    def stat_copy(q):
        return remote(
            stat_out.at[q], stat_in.at[q], stat_send.at[q], stat_recv.at[q], device(OFFSETS[q])
        )

    def norm_copy(q):
        return remote(
            norm.at[0], norm.at[q], norm_send.at[q], norm_recv.at[q], device(OFFSETS[q], -1)
        )

    for q in FAR_FIRST:
        for m in range(2):
            stat_out[q, 2 * m : 2 * m + 2, :] = stat[q, m, 0:2, :]
        stat_copy(q).start()
    for q in range(1, SLOTS):
        stat_copy(q).wait_recv()
    for m in range(2):
        tops = [stat[0, m, 0:1, :]] + [stat_in[q, 2 * m : 2 * m + 1, :] for q in range(1, SLOTS)]
        sums = [stat[0, m, 1:2, :]] + [stat_in[q, 2 * m + 1 : 2 * m + 2, :] for q in range(1, SLOTS)]
        top = functools.reduce(jnp.maximum, tops)
        both[2 * m : 2 * m + 1, :] = top
        both[2 * m + 1 : 2 * m + 2, :] = sum(s * jnp.exp2(t - top) for t, s in zip(tops, sums))
    both_copy = remote(both, both_in, both_send, both_recv, sibling)
    both_copy.start()
    both_copy.wait_recv()
    for m in range(2):
        one, two_ = both[2 * m : 2 * m + 1, :], both_in[2 * m : 2 * m + 1, :]
        top = jnp.maximum(one, two_)
        norm[0, m : m + 1, :] = top + jnp.log2(
            both[2 * m + 1 : 2 * m + 2, :] * jnp.exp2(one - top)
            + both_in[2 * m + 1 : 2 * m + 2, :] * jnp.exp2(two_ - top)
        )
    for q in FAR_FIRST:
        norm_copy(q).start()
    for q in range(1, SLOTS):
        norm_copy(q).wait_recv()

    def half_copy(q):
        return remote(acc.at[q, other], half_in.at[q], half_send.at[q], half_recv.at[q], sibling)

    def part_copy(q, c):
        size = shard // SUM_PIECES
        return remote(
            acc.at[q, core, pl.ds(c * size, size)], part_in.at[q, pl.ds(c * size, size)],
            part_send.at[q, c], part_recv.at[q, c], device(sum_edge(q, c)),
        )

    def pass_on(q, c):
        if (q, c) in FIRST:
            half_copy(q).wait_recv()
        elif q:
            part_copy(q, 1 - c).wait_send()
        size = shard // SUM_PIECES
        at = pl.ds(c * size, size)
        total = acc[q, core, at] + half_in[q, at]
        for child in range(1, SLOTS):
            if GOES_TO[child, c] == q:
                part_copy(child, c).wait_recv()
                total = total + part_in[child, at]
        if q:
            acc[q, core, at] = total
            part_copy(q, c).start()
        else:
            o_ref[at] = scale * total

    def column_of(line):
        return jnp.concatenate([jnp.transpose(jnp.broadcast_to(line, (128, full)))] * (wide // 128), axis=1)

    def differences(code, par):
        a, b1, b2 = ends(code)
        n = field(code, 15, 4)
        left = [column_of(norm[a, m : m + 1, :]) for m in range(2)]
        top = [
            jnp.concatenate([norm[b1, m : m + 1, :], norm[b2, m : m + 1, :]], axis=1) for m in range(2)
        ]
        zt, zs = z[n], z[ITEMS + n]
        diff[par, 0] = (jnp.exp2(zs - left[1]) - jnp.exp2(zt - left[0])).astype(BF16)
        diff[par, 1] = (jnp.exp2(zs - top[1]) - jnp.exp2(zt - top[0])).astype(BF16)

    def products(code, par):
        a, b1, b2 = ends(code)
        by_row, by_col = diff[par, 0], diff[par, 1]
        sa, sb = block(a, 1), two(b1, b2, 1)
        forward = jnp.dot(
            jnp.concatenate([by_row, by_col], axis=1), jnp.concatenate([sb, sb], axis=0),
            preferred_element_type=F32,
        )
        acc[a] = acc[a] + forward.reshape(2, shard, width)
        backward = lax.dot_general(
            jnp.concatenate([by_row, by_col], axis=0), jnp.concatenate([sa, sa], axis=0),
            (((0,), (0,)), ((), ())), preferred_element_type=F32,
        )
        acc[b1] = acc[b1] + backward[:full].reshape(2, shard, width)
        acc[b2] = acc[b2] + backward[full:].reshape(2, shard, width)

    def after(step):
        for q in reversed(range(SLOTS)):
            if q and DONE[q] == step:
                half_copy(q).start()
        for q, c in PASS_ON.get(step, ()):
            pass_on(q, c)

    first = look_up(ITEM_CODES, core, ITEMS - 1)
    differences(first, 0)

    def second_pass(h, code):
        for par in range(2):
            later = look_up(ITEM_CODES, core, ITEMS - 2 - (2 * h + par))
            differences(later, 1 - par)
            products(code, par)
            code = later
            for step in range(par, ITEMS - 1, 2):
                if step in DONE or step in PASS_ON:
                    @pl.when(h == step // 2)
                    def _(step=step):
                        after(step)
        return code

    last = lax.fori_loop(0, (ITEMS - 1) // 2, second_pass, first)
    products(last, 0)
    after(ITEMS - 1)
    for q, c in LAST:
        pass_on(q, c)
        if (q, c) == OWN_HALF_AFTER:
            half_copy(0).start()

    both_copy.wait_send()
    for q in range(SLOTS):
        for m in range(2):
            for c in range(ROW_PIECES):
                if q and (PARENT[q] or m == 1 and c == ROW_PIECES - 1):
                    tree(q, m, c).wait_send()
                across(q, m, c).wait_send()
        half_copy(q).wait_send()
        if q:
            stat_copy(q).wait_send()
            norm_copy(q).wait_send()
            part_copy(*SECOND[q]).wait_send()


def on_device(teacher, student):
    shard, width = teacher.shape
    full = 2 * shard
    dma = pltpu.SemaphoreType.DMA
    return pl.pallas_call(
        kernel,
        out_shape=jax.ShapeDtypeStruct((shard, width), F32),
        in_specs=[pl.BlockSpec(memory_space=pltpu.VMEM)] * 2,
        out_specs=pl.BlockSpec(memory_space=pltpu.VMEM),
        scratch_shapes=[
            pltpu.VMEM((SLOTS, 2, 2, shard, width), BF16),
            pltpu.VMEM((STEPS, full, 2 * full), F32),
            pltpu.VMEM((SLOTS, 2, shard, width), F32),
            pltpu.VMEM((2, full, 2 * full), F32),
            pltpu.VMEM((2, 2, full, 2 * full), BF16),
            pltpu.VMEM((128, 128), F32),
            pltpu.VMEM((SLOTS, 2, 8, full), F32),
            pltpu.VMEM((SLOTS, 4, full), F32),
            pltpu.VMEM((SLOTS, 4, full), F32),
            pltpu.VMEM((4, full), F32),
            pltpu.VMEM((4, full), F32),
            pltpu.VMEM((SLOTS, 2, full), F32),
            pltpu.VMEM((SLOTS, shard, width), F32),
            pltpu.VMEM((SLOTS, shard, width), F32),
            dma((SLOTS, 2, ROW_PIECES)), dma((SLOTS, 2, ROW_PIECES)),
            dma((SLOTS, 2, ROW_PIECES)), dma((SLOTS, 2, ROW_PIECES)),
            dma((SLOTS,)), dma((SLOTS,)), dma, dma,
            dma((SLOTS,)), dma((SLOTS,)), dma((SLOTS,)), dma((SLOTS,)),
            dma((SLOTS, SUM_PIECES)), dma((SLOTS, SUM_PIECES)),
        ],
        compiler_params=pltpu.CompilerParams(
            collective_id=0, has_side_effects=True, vmem_limit_bytes=62 * 1024 * 1024
        ),
    )(teacher, student)


def solution(mesh):
    return jax.shard_map(
        on_device,
        mesh=mesh,
        in_specs=(P(("row", "col"), None), P(("row", "col"), None)),
        out_specs=P(("row", "col"), None),
        check_vma=False,
    )
```

```python
import functools
import math

import jax
import jax.numpy as jnp
from jax import lax
from jax.experimental import pallas as pl
from jax.experimental.pallas import tpu as pltpu
from jax.sharding import PartitionSpec as P

F32 = jnp.float32
BF16 = jnp.bfloat16
MESH = pl.DeviceIdType.MESH
SIDE = 4

OFFSETS = (
    (0, 0, 0), (3, 0, 0), (0, 0, 1), (1, 0, 0), (0, 3, 3), (3, 1, 0),
    (1, 0, 1), (0, 2, 3), (3, 2, 0), (3, 1, 3), (1, 0, 2),
)
PARENT = (None, 0, 0, 0, 0, 1, 2, 4, 5, 5, 6)
SLOTS = len(OFFSETS)
CHILDREN = tuple(tuple(q for q in range(SLOTS) if PARENT[q] == p) for p in range(SLOTS))
LEVEL = []
for parent in PARENT:
    LEVEL.append(0 if parent is None else LEVEL[parent] + 1)
LEVELS = tuple(tuple(q for q in range(SLOTS) if LEVEL[q] == level) for level in range(4))

WORK = (
    (
        (2, 1, 0), (4, 3, 2),
        (1, 6, 5), (6, 5, 4), (7, 3, 0),
        (9, 7, 6), (0, 10, 5), (10, 3, 1), (10, 9, 8),
    ),
    (
        (0, 0, 1), (3, 2, 1), (4, 1, 0),
        (5, 4, 3), (2, 7, 5), (7, 6, 5),
        (9, 2, 1), (8, 1, 0), (8, 6, 3),
    ),
)
ITEMS = len(WORK[0])
STEPS = 2 * ITEMS
ROW_PIECES = 1
SUM_PIECES = 2


def minus(a, b):
    return tuple((p - q) % SIDE for p, q in zip(a, b))


def is_half(a, b):
    d = minus(OFFSETS[a], OFFSETS[b])
    return d == minus((0, 0, 0), d)


def check_work():
    found = [
        min(minus(OFFSETS[a], OFFSETS[b]), minus(OFFSETS[b], OFFSETS[a]))
        for work in WORK
        for a, b1, b2 in work
        for b in (b1, b2)
    ]
    assert len(found) == len(set(found)) == (SIDE**3 + 8) // 2


check_work()


def group_of(item, m):
    return max(max(LEVEL[q] for q in item), 1) - 1 + m


def sequence(core):
    steps = [(group_of(item, m), m, n) for n, item in enumerate(WORK[core]) for m in range(2)]
    return tuple((m, n) for _, m, n in sorted(steps))


SEQUENCE = (sequence(0), sequence(1))
GROUP_START = tuple(
    min(
        min(s for s, (m, n) in enumerate(SEQUENCE[core]) if group_of(WORK[core][n], m) == g)
        for core in range(2)
    )
    for g in range(4)
)
TAKEN = {-1: ((0, 1), (1, 0), (1, 1), (2, 0)), 1: ((2, 1), (3, 0)), 9: ((3, 1),)}
HANDED = {-1: ((0, 0), (1, 0)), 1: ((2, 0), (0, 1), (1, 1)), 5: ((3, 0),), 9: ((2, 1),), 13: ((3, 1),)}
assert GROUP_START == (0, 2, 7, 14)


def packed(item, m, n):
    a, b1, b2 = item
    return (
        a + b1 * 16 + b2 * 256 + int(is_half(a, b1)) * 4096 + int(is_half(a, b2)) * 8192
        + m * 16384 + n * 32768
    )


STEP_CODES = tuple(tuple(packed(WORK[c][n], m, n) for m, n in SEQUENCE[c]) for c in range(2))
ITEM_CODES = tuple(tuple(packed(item, 0, n) for n, item in enumerate(WORK[c])) for c in range(2))


def look_up(codes, core, at):
    value = jnp.int32(0)
    for n, (one, two) in enumerate(zip(*codes)):
        value = jnp.where(at == n, jnp.where(core == 0, jnp.int32(one), jnp.int32(two)), value)
    return value


def field(code, start, bits):
    return (code >> start) & ((1 << bits) - 1)


FAR_FIRST = tuple(sorted(range(1, SLOTS), key=lambda q: -sum(min(d, SIDE - d) for d in OFFSETS[q])))

DONE = tuple(
    max(ITEMS - 1 - n for work in WORK for n, item in enumerate(work) if q in item)
    for q in range(SLOTS)
)
GOES_TO = {(q, c): PARENT[q] for q in range(1, SLOTS) for c in range(SUM_PIECES)}
GOES_TO[5, 1] = 0
GOES_TO[6, 0] = 3
PASS_ON = {
    3: ((8, 0), (10, 0)), 4: ((9, 0),), 5: ((8, 1), (10, 1), (7, 0)), 6: ((9, 1),), 7: ((7, 1),),
}
LAST = (
    (6, 0), (4, 0), (3, 1), (5, 0), (1, 1), (2, 0), (6, 1), (4, 1), (5, 1), (3, 0), (1, 0), (2, 1), (0, 0), (0, 1),
)
OWN_HALF_AFTER = (2, 0)
ORDER = tuple(piece for step in sorted(PASS_ON) for piece in PASS_ON[step]) + LAST
FIRST = tuple(next(piece for piece in ORDER if piece[0] == q) for q in range(SLOTS))
SECOND = tuple(next(piece for piece in ORDER[::-1] if piece[0] == q) for q in range(SLOTS))
assert len(set(ORDER)) == len(ORDER) == SLOTS * SUM_PIECES == 2 * SLOTS


def kernel(
    t_ref, s_ref, o_ref, rows, z, acc, tile, diff, pen, stat, stat_out, stat_in, both, both_in, norm,
    half_in, part_in,
    tree_send, tree_recv, pair_send, pair_recv, stat_send, stat_recv, both_send, both_recv,
    norm_send, norm_recv, half_send, half_recv, part_send, part_recv,
):
    shard, width = t_ref.shape
    full = 2 * shard
    wide = 2 * full
    scale = 1.0 / (0.1 * math.sqrt(width))
    row = lax.axis_index("row")
    col = lax.axis_index("col")
    core = row & 1
    other = 1 - core
    x, y, zz = col & 3, (row >> 1) & 3, ((col >> 2) << 1) + (row >> 3)
    places = {}

    def device(d, sign=1):
        d = tuple((sign * q) % SIDE for q in d)
        if d not in places:
            to = [(p + q) & 3 if q else p for p, q in zip((x, y, zz), d)]
            places[d] = (((to[2] & 1) << 3) + (to[1] << 1) + core, ((to[2] >> 1) << 2) + to[0])
        return places[d]

    sibling = (row ^ 1, col)

    def edge(q):
        return minus(OFFSETS[q], OFFSETS[PARENT[q]])

    def sum_edge(q, c):
        return minus(OFFSETS[q], OFFSETS[GOES_TO[q, c]])

    partners = set()
    for q in range(1, SLOTS):
        for d in [OFFSETS[q], edge(q)] + [sum_edge(q, c) for c in range(SUM_PIECES)]:
            partners.add(d)
            partners.add(minus((0, 0, 0), d))
    partners = sorted(partners)

    barrier = pltpu.get_barrier_semaphore()
    for d in partners:
        pl.semaphore_signal(barrier, inc=1, device_id=device(d), device_id_type=MESH)
    pl.semaphore_signal(barrier, inc=1, device_id=sibling, device_id_type=MESH)
    rows[0, 0, core] = t_ref[...]
    rows[0, 1, core] = s_ref[...]

    def remote(src, dst, send, recv, to):
        return pltpu.make_async_remote_copy(
            src_ref=src, dst_ref=dst, send_sem=send, recv_sem=recv, device_id=to, device_id_type=MESH
        )

    def piece(q, m, c):
        size = shard // ROW_PIECES
        return rows.at[q, m, core, pl.ds(c * size, size)]

    def tree(q, m, c):
        return remote(
            piece(PARENT[q], m, c), piece(q, m, c), tree_send.at[q, m, c], tree_recv.at[q, m, c],
            device(edge(q), -1),
        )

    def across(q, m, c):
        part = piece(q, m, c)
        return remote(part, part, pair_send.at[q, m, c], pair_recv.at[q, m, c], sibling)

    def take_up(level, n):
        m, c = n // ROW_PIECES, n % ROW_PIECES
        if level == 0 and n:
            for child in CHILDREN[0]:
                tree(child, (n - 1) // ROW_PIECES, (n - 1) % ROW_PIECES).wait_send()
        for q in LEVELS[level]:
            if q:
                tree(q, m, c).wait_recv()
            for child in sorted(CHILDREN[q], key=lambda p: not CHILDREN[p]):
                tree(child, m, c).start()
        for q in LEVELS[level]:
            across(q, m, c).start()

    def arrive(level, m):
        for q in LEVELS[level]:
            for c in range(ROW_PIECES):
                across(q, m, c).wait_recv()

    def before(step):
        for level, n in TAKEN.get(step, ()):
            take_up(level, n)
        for level, m in HANDED.get(step, ()):
            arrive(level, m)

    pl.semaphore_wait(barrier, len(partners) + 1)
    take_up(0, 0)

    acc[...] = jnp.zeros_like(acc)
    for m in range(2):
        stat[:, m, 0:1, :] = jnp.full((SLOTS, 1, full), -1e30, F32)
        stat[:, m, 1:2, :] = jnp.zeros((SLOTS, 1, full), F32)
    pen[...] = jnp.where(
        lax.broadcasted_iota(jnp.int32, (128, 128), 0) == lax.broadcasted_iota(jnp.int32, (128, 128), 1),
        F32(-1e30), F32(0.0),
    )

    def block(q, m):
        return rows[q, m].reshape(full, width)

    def two(b1, b2, m):
        return jnp.concatenate([block(b1, m), block(b2, m)], axis=0)

    def ends(code):
        return field(code, 0, 4), field(code, 4, 4), field(code, 8, 4)

    def scores(code, par):
        a, b1, b2 = ends(code)
        m = field(code, 14, 1)
        less = [jnp.full((1, full), field(code, bit, 1).astype(F32)) for bit in (12, 13)]
        tile[par] = lax.dot_general(
            block(a, m), two(b1, b2, m), (((1,), (1,)), ((), ())), preferred_element_type=F32
        ) * (scale * math.log2(math.e)) - jnp.concatenate(less, axis=1)
        own = (a == b1).astype(F32)
        for k in range(0, full, 128):
            tile[par, k : k + 128, k : k + 128] += pen[...] * own

    def merge(ref, top, total):
        old = ref[0:1, :]
        new = jnp.maximum(old, top)
        ref[1:2, :] = ref[1:2, :] * jnp.exp2(old - new) + total * jnp.exp2(top - new)
        ref[0:1, :] = new

    def lanes(value):
        return [value[:, j : j + 128] for j in range(0, wide, 128)]

    def statistics(code, par):
        a, b1, b2 = ends(code)
        m = field(code, 14, 1)
        at = m * ITEMS + field(code, 15, 4)
        right, down = [], None
        for k in range(0, full, 128):
            score = tile[par, k : k + 128, :]
            z[at, k : k + 128, :] = score
            most = functools.reduce(jnp.maximum, lanes(score))
            right.append(jnp.max(jnp.transpose(most), axis=0, keepdims=True))
            most = jnp.max(score.reshape(16, 8, wide), axis=0)
            down = most if down is None else jnp.maximum(down, most)
        down = jnp.max(down, axis=0, keepdims=True)
        right = jnp.concatenate(right, axis=1)
        column = jnp.transpose(jnp.broadcast_to(right, (128, full)))
        right_sum, down_sum = [], None
        for k in range(0, full, 128):
            score = tile[par, k : k + 128, :]
            across_ = sum(jnp.exp2(part - column[k : k + 128]) for part in lanes(score))
            right_sum.append(jnp.sum(jnp.transpose(across_), axis=0, keepdims=True))
            below = jnp.sum(jnp.exp2(score - down).reshape(16, 8, wide), axis=0)
            down_sum = below if down_sum is None else down_sum + below
        down_sum = jnp.sum(down_sum, axis=0, keepdims=True)
        merge(stat.at[a, m], right, jnp.concatenate(right_sum, axis=1))
        merge(stat.at[b1, m], down[:, :full], down_sum[:, :full])
        merge(stat.at[b2, m], down[:, full:], down_sum[:, full:])

    before(-1)
    first, second = look_up(STEP_CODES, core, 0), look_up(STEP_CODES, core, 1)
    scores(first, 0)
    scores(second, 1)
    statistics(first, 0)

    def first_pass(h, code):
        for step in sorted(set(TAKEN) | set(HANDED)):
            if step >= 0:
                @pl.when(2 * h + 1 == step)
                def _(step=step):
                    before(step)
        for par in (1, 0):
            later = look_up(STEP_CODES, core, 2 * h + 3 - par)
            scores(later, 1 - par)
            statistics(code, par)
            code = later
        return code

    statistics(lax.fori_loop(0, STEPS // 2 - 1, first_pass, second), 1)

    def stat_copy(q):
        return remote(
            stat_out.at[q], stat_in.at[q], stat_send.at[q], stat_recv.at[q], device(OFFSETS[q])
        )

    def norm_copy(q):
        return remote(
            norm.at[0], norm.at[q], norm_send.at[q], norm_recv.at[q], device(OFFSETS[q], -1)
        )

    for q in FAR_FIRST:
        for m in range(2):
            stat_out[q, 2 * m : 2 * m + 2, :] = stat[q, m, 0:2, :]
        stat_copy(q).start()
    for q in range(1, SLOTS):
        stat_copy(q).wait_recv()
    for m in range(2):
        tops = [stat[0, m, 0:1, :]] + [stat_in[q, 2 * m : 2 * m + 1, :] for q in range(1, SLOTS)]
        sums = [stat[0, m, 1:2, :]] + [stat_in[q, 2 * m + 1 : 2 * m + 2, :] for q in range(1, SLOTS)]
        top = functools.reduce(jnp.maximum, tops)
        both[2 * m : 2 * m + 1, :] = top
        both[2 * m + 1 : 2 * m + 2, :] = sum(s * jnp.exp2(t - top) for t, s in zip(tops, sums))
    both_copy = remote(both, both_in, both_send, both_recv, sibling)
    both_copy.start()
    both_copy.wait_recv()
    for m in range(2):
        one, two_ = both[2 * m : 2 * m + 1, :], both_in[2 * m : 2 * m + 1, :]
        top = jnp.maximum(one, two_)
        norm[0, m : m + 1, :] = top + jnp.log2(
            both[2 * m + 1 : 2 * m + 2, :] * jnp.exp2(one - top)
            + both_in[2 * m + 1 : 2 * m + 2, :] * jnp.exp2(two_ - top)
        )
    for q in FAR_FIRST:
        norm_copy(q).start()
    for q in range(1, SLOTS):
        norm_copy(q).wait_recv()

    def half_copy(q):
        return remote(acc.at[q, other], half_in.at[q], half_send.at[q], half_recv.at[q], sibling)

    def part_copy(q, c):
        size = shard // SUM_PIECES
        return remote(
            acc.at[q, core, pl.ds(c * size, size)], part_in.at[q, pl.ds(c * size, size)],
            part_send.at[q, c], part_recv.at[q, c], device(sum_edge(q, c)),
        )

    def pass_on(q, c):
        if (q, c) in FIRST:
            half_copy(q).wait_recv()
        elif q:
            part_copy(q, 1 - c).wait_send()
        size = shard // SUM_PIECES
        at = pl.ds(c * size, size)
        total = acc[q, core, at] + half_in[q, at]
        for child in range(1, SLOTS):
            if GOES_TO[child, c] == q:
                part_copy(child, c).wait_recv()
                total = total + part_in[child, at]
        if q:
            acc[q, core, at] = total
            part_copy(q, c).start()
        else:
            o_ref[at] = scale * total

    def column_of(line):
        return jnp.concatenate([jnp.transpose(jnp.broadcast_to(line, (128, full)))] * (wide // 128), axis=1)

    def differences(code, par):
        a, b1, b2 = ends(code)
        n = field(code, 15, 4)
        left = [column_of(norm[a, m : m + 1, :]) for m in range(2)]
        top = [
            jnp.concatenate([norm[b1, m : m + 1, :], norm[b2, m : m + 1, :]], axis=1) for m in range(2)
        ]
        zt, zs = z[n], z[ITEMS + n]
        diff[par, 0] = (jnp.exp2(zs - left[1]) - jnp.exp2(zt - left[0])).astype(BF16)
        diff[par, 1] = (jnp.exp2(zs - top[1]) - jnp.exp2(zt - top[0])).astype(BF16)

    def products(code, par):
        a, b1, b2 = ends(code)
        by_row, by_col = diff[par, 0], diff[par, 1]
        sa, sb = block(a, 1), two(b1, b2, 1)
        forward = jnp.dot(
            jnp.concatenate([by_row, by_col], axis=1), jnp.concatenate([sb, sb], axis=0),
            preferred_element_type=F32,
        )
        acc[a] = acc[a] + forward.reshape(2, shard, width)
        backward = lax.dot_general(
            jnp.concatenate([by_row, by_col], axis=0), jnp.concatenate([sa, sa], axis=0),
            (((0,), (0,)), ((), ())), preferred_element_type=F32,
        )
        acc[b1] = acc[b1] + backward[:full].reshape(2, shard, width)
        acc[b2] = acc[b2] + backward[full:].reshape(2, shard, width)

    def after(step):
        for q in reversed(range(SLOTS)):
            if q and DONE[q] == step:
                half_copy(q).start()
        for q, c in PASS_ON.get(step, ()):
            pass_on(q, c)

    first = look_up(ITEM_CODES, core, ITEMS - 1)
    differences(first, 0)

    def second_pass(h, code):
        for par in range(2):
            later = look_up(ITEM_CODES, core, ITEMS - 2 - (2 * h + par))
            differences(later, 1 - par)
            products(code, par)
            code = later
            for step in range(par, ITEMS - 1, 2):
                if step in DONE or step in PASS_ON:
                    @pl.when(h == step // 2)
                    def _(step=step):
                        after(step)
        return code

    last = lax.fori_loop(0, (ITEMS - 1) // 2, second_pass, first)
    products(last, 0)
    after(ITEMS - 1)
    for q, c in LAST:
        pass_on(q, c)
        if (q, c) == OWN_HALF_AFTER:
            half_copy(0).start()

    both_copy.wait_send()
    for q in range(SLOTS):
        for m in range(2):
            for c in range(ROW_PIECES):
                if q and (PARENT[q] or m == 1 and c == ROW_PIECES - 1):
                    tree(q, m, c).wait_send()
                across(q, m, c).wait_send()
        half_copy(q).wait_send()
        if q:
            stat_copy(q).wait_send()
            norm_copy(q).wait_send()
            part_copy(*SECOND[q]).wait_send()


def on_device(teacher, student):
    shard, width = teacher.shape
    full = 2 * shard
    dma = pltpu.SemaphoreType.DMA
    return pl.pallas_call(
        kernel,
        out_shape=jax.ShapeDtypeStruct((shard, width), F32),
        in_specs=[pl.BlockSpec(memory_space=pltpu.VMEM)] * 2,
        out_specs=pl.BlockSpec(memory_space=pltpu.VMEM),
        scratch_shapes=[
            pltpu.VMEM((SLOTS, 2, 2, shard, width), BF16),
            pltpu.VMEM((STEPS, full, 2 * full), F32),
            pltpu.VMEM((SLOTS, 2, shard, width), F32),
            pltpu.VMEM((2, full, 2 * full), F32),
            pltpu.VMEM((2, 2, full, 2 * full), BF16),
            pltpu.VMEM((128, 128), F32),
            pltpu.VMEM((SLOTS, 2, 8, full), F32),
            pltpu.VMEM((SLOTS, 4, full), F32),
            pltpu.VMEM((SLOTS, 4, full), F32),
            pltpu.VMEM((4, full), F32),
            pltpu.VMEM((4, full), F32),
            pltpu.VMEM((SLOTS, 2, full), F32),
            pltpu.VMEM((SLOTS, shard, width), F32),
            pltpu.VMEM((SLOTS, shard, width), F32),
            dma((SLOTS, 2, ROW_PIECES)), dma((SLOTS, 2, ROW_PIECES)),
            dma((SLOTS, 2, ROW_PIECES)), dma((SLOTS, 2, ROW_PIECES)),
            dma((SLOTS,)), dma((SLOTS,)), dma, dma,
            dma((SLOTS,)), dma((SLOTS,)), dma((SLOTS,)), dma((SLOTS,)),
            dma((SLOTS, SUM_PIECES)), dma((SLOTS, SUM_PIECES)),
        ],
        compiler_params=pltpu.CompilerParams(
            collective_id=0, has_side_effects=True, vmem_limit_bytes=62 * 1024 * 1024
        ),
    )(teacher, student)


def solution(mesh):
    return jax.shard_map(
        on_device,
        mesh=mesh,
        in_specs=(P(("row", "col"), None), P(("row", "col"), None)),
        out_specs=P(("row", "col"), None),
        check_vma=False,
    )
```
